32 devices in a mesh: groups: 2 (over y), wband: 2 (over core), tile: 8 (over z, x).
Axes of the slice: x: 2, y: 2, z: 4, core: 2. Of those that a mesh axis runs over, the one named last changes fastest.
Arguments:
- visibility: float32 [65536, 2], P(('groups', 'wband', 'tile')), parts along dimension 0, may hold values from -6 to 6
- plane_index: int32 [65536], P(('groups', 'wband', 'tile')), parts along dimension 0, may hold values from 0 to 63, as said below
- beam_index: int32 [65536], P(('groups', 'wband', 'tile')), parts along dimension 0, may hold values from 0 to 31
- strip_index: int32 [65536], P(('groups', 'wband', 'tile')), parts along dimension 0, may hold values from 0 to 7, as said below
- cell_row: int32 [65536], P(('groups', 'wband', 'tile')), parts along dimension 0, may hold values from 0 to 63
- cell_column: int32 [65536], P(('groups', 'wband', 'tile')), parts along dimension 0, may hold values from 0 to 8184
- phase_index: int32 [65536], P(('groups', 'wband', 'tile')), parts along dimension 0, may hold values from 0 to 63, as said below
- kernel_table: bfloat16 [64, 32, 64, 128], P('wband', None, 'tile'), may hold values from -6 to 6
Outputs:
- grid: float32 [2, 1024, 8192], P(None, ('groups', 'tile'), 'wband'), parts along dimension 1
The draws below stay inside these ranges and needn't reach their ends.
There are 2 independent parts, one for each index of `groups`. The reference program is written for one: setup_inputs(seed, part) draws one part's arguments, and reference() takes and returns one part's arrays. A program takes and returns all parts, laid end to end along the dimension named above; an argument that names none is the same for every part. Nothing has to cross between parts.
Inputs may be any that keep to these rules, and one draw needn't show every extreme that they name: `plane_index`: the blocks at wband index b have w-planes from b * 32 to (b + 1) * 32 - 1. `strip_index`: among the 2048 blocks of one device, at most 512 land in any one strip. `phase_index`: among the 2048 blocks of one device, at most 64 have any one phase.
All inputs are finite; a program needn't handle non-finite values.
Results may differ from the reference program's by a relative error of at most 0.003.
Values may be sent and summed in bfloat16 or wider, within the bound.
A program may use at most 192 MiB of HBM per device.

```python
import jax
import jax.numpy as jnp
from jax import lax

SUP = 8
PHASES = 64
WPLANES = 64
BEAMS = 32
NV = 8192
ROWS = 64
BLK_DEV = 2048
WB = 32
STRIPS = 8
NU = 512
BLOCKS = 32768
CAP_STRIP = 512
CAP_PHASE = 64


def capped_targets(key, per_source, targets, capacity, sources):
    hottest = jax.random.randint(jax.random.fold_in(key, 1), (), 0, targets)
    remainder = jnp.arange((targets - 1) * capacity, dtype=jnp.int32) // capacity
    remainder = remainder + (remainder >= hottest).astype(jnp.int32)

    def one_source(source_key):
        first_key, second_key = jax.random.split(source_key)
        mixed = jax.random.permutation(first_key, remainder)[:per_source - capacity]
        listing = jnp.concatenate([jnp.zeros((capacity,), jnp.int32) + hottest, mixed])
        return jax.random.permutation(second_key, listing)
    source_keys = jax.random.split(jax.random.fold_in(key, 2), sources)
    return jax.vmap(one_source)(source_keys).reshape(-1).astype(jnp.int32)


def draw_strip_index(key, part):
    key = jax.random.fold_in(key, 11)
    return capped_targets(key, BLK_DEV, STRIPS, CAP_STRIP, BLOCKS // BLK_DEV)


def draw_phase_index(key, part):
    key = jax.random.fold_in(key, 12)
    return capped_targets(key, BLK_DEV, PHASES, CAP_PHASE, BLOCKS // BLK_DEV)


def draw_plane_index(key, part):
    key = jax.random.fold_in(key, 13)
    positions = jnp.arange(BLOCKS, dtype=jnp.int32)
    band_number = positions // (BLK_DEV * STRIPS)
    return (band_number * WB + jax.random.randint(key, (BLOCKS,), 0, WB)).astype(jnp.int32)


def set_ends(values, rng, low, largest):
    longest = values.shape.index(max(values.shape))
    spots = []
    for shift in (0, 1):
        where = [jax.random.randint(jax.random.fold_in(rng, axis), (), 0, length) for axis, length in enumerate(values.shape)]
        where[longest] = (where[longest] + shift) % values.shape[longest]
        spots.append(tuple(where))
    return values.at[spots[0]].set(low).at[spots[1]].set(largest)


def shard_levels(rng, shape, shards, least, largest):
    factor_of, own = 1.0, jax.random.fold_in(rng, 6)
    for axis_at, shards_of in shards:
        draws = jnp.exp(jax.random.uniform(jax.random.fold_in(own, axis_at), (shards_of,), jnp.float32, least / len(shards), largest / len(shards)))
        factor_of = factor_of * jnp.repeat(draws, shape[axis_at] // shards_of).reshape([-1 if axis == axis_at else 1 for axis in range(len(shape))])
    return factor_of


def centred(rng, dims, scale, reach, shards=(), kind=jnp.bfloat16):
    result = scale * jax.random.normal(rng, dims, jnp.float32)
    if shards:
        result = result * shard_levels(rng, dims, shards, -0.22, 0.18)
    return jnp.clip(result, -reach, reach).astype(kind)


def setup_inputs(seed: int = 0, part: int = 0) -> dict:
    arg_keys = jax.random.split(jax.random.key(seed), 9)
    part_splits = jax.random.split(jax.random.fold_in(arg_keys[8], part), 9)
    return {
        "visibility": centred(part_splits[0], (BLOCKS, 2), 1.0, 6.0, ((0, 16),), jnp.float32),
        "plane_index": draw_plane_index(jax.random.fold_in(jax.random.fold_in(arg_keys[8], part), 71), part),
        "beam_index": set_ends(jax.random.randint(part_splits[2], (BLOCKS,), 0, BEAMS), jax.random.fold_in(part_splits[2], 1), 0, BEAMS - 1).astype(jnp.int32),
        "strip_index": draw_strip_index(jax.random.fold_in(jax.random.fold_in(arg_keys[8], part), 71), part),
        "cell_row": set_ends(jax.random.randint(part_splits[4], (BLOCKS,), 0, ROWS), jax.random.fold_in(part_splits[4], 1), 0, ROWS - 1).astype(jnp.int32),
        "cell_column": set_ends(jax.random.randint(part_splits[5], (BLOCKS,), 0, NV - SUP + 1), jax.random.fold_in(part_splits[5], 1), 0, NV - SUP).astype(jnp.int32),
        "phase_index": draw_phase_index(jax.random.fold_in(jax.random.fold_in(arg_keys[8], part), 71), part),
        "kernel_table": centred(arg_keys[7], (WPLANES, BEAMS, PHASES, 2 * SUP * SUP), 1.0, 6.0, ((0, 2), (2, 8))),
    }


def make_patches(values, kernel_rows):
    widened = kernel_rows.astype(jnp.float32)
    halfway = widened.shape[1] // 2
    real_kernel = widened[:, :halfway]
    imag_kernel = widened[:, halfway:]
    real_value = values[:, 0:1]
    imag_value = values[:, 1:2]
    real_part = real_value * real_kernel - imag_value * imag_kernel
    imag_part = real_value * imag_kernel + imag_value * real_kernel
    return jnp.concatenate([real_part, imag_part], axis=1).astype(jnp.bfloat16)


def cell_index(row_start, col_start, columns, height, support):
    component = jnp.arange(2, dtype=jnp.int32)[None, :, None, None]
    across = jnp.arange(support, dtype=jnp.int32)
    flat_index = (component * height + row_start[:, None, None, None] + across[None, None, :, None]) * columns
    return flat_index + col_start[:, None, None, None] + across[None, None, None, :]


def reference(visibility, plane_index, beam_index, strip_index, cell_row, cell_column, phase_index, kernel_table):
    flat_table = kernel_table.reshape(WPLANES * BEAMS * PHASES, 2 * SUP * SUP)
    height = NU + SUP - 1

    def window_of(source, number):
        return lax.dynamic_slice_in_dim(source, number * BLK_DEV, BLK_DEV, 0)

    def gridding(number, canvas):
        values = window_of(visibility, number)
        lookup = (window_of(plane_index, number) * BEAMS + window_of(beam_index, number)) * PHASES + window_of(phase_index, number)
        patches = make_patches(values, flat_table[lookup])
        row_start = window_of(strip_index, number) * ROWS + window_of(cell_row, number)
        flat_index = cell_index(row_start, window_of(cell_column, number), NV, height, SUP)
        return canvas.at[flat_index.reshape(-1)].add(patches.astype(jnp.float32).reshape(-1))

    canvas = jnp.zeros((2 * height * NV,), jnp.float32)
    canvas = lax.fori_loop(0, BLOCKS // BLK_DEV, gridding, canvas)
    return canvas.reshape(2, height, NV)[:, :NU, :]
```

```python
import functools

import jax
import jax.numpy as jnp
from jax import lax
from jax.experimental import pallas as pl
from jax.experimental.pallas import tpu as pltpu
from jax.sharding import PartitionSpec as P

SUP = 8
NV = 8192
ROWS = 64
LANES = 128
HALF = LANES // 2
SHIFT = 5
STRIDE = 1 << SHIFT
HEIGHT = ROWS + SUP
TILES = NV // STRIDE + 1
CHAINS = 2


def rank_in_bucket(target, buckets):
    onehot = (target[:, None] == jnp.arange(buckets, dtype=jnp.int32)[None, :]).astype(jnp.int32)
    ranking = jnp.cumsum(onehot, axis=0) - 1
    return jnp.sum(ranking * onehot, axis=1)


def fetch_kernel(unroll, keys_ref, table_ref, out_ref, wide, picked):
    wide[...] = table_ref[...].astype(jnp.float32)

    def body(i, carry):
        for u in range(unroll):
            n = i * unroll + u
            picked[pl.ds(n, 1), :] = wide[pl.ds(keys_ref[n], 1), :]
        return carry

    lax.fori_loop(0, out_ref.shape[0] // unroll, body, 0)
    out_ref[...] = picked[...].astype(jnp.bfloat16)


def fetch_rows(keys, table):
    total, width = keys.shape[0], table.shape[1]
    return pl.pallas_call(
        functools.partial(fetch_kernel, 16),
        out_shape=jax.ShapeDtypeStruct((total, width), jnp.bfloat16),
        in_specs=[
            pl.BlockSpec(memory_space=pltpu.SMEM),
            pl.BlockSpec(memory_space=pltpu.VMEM),
        ],
        out_specs=pl.BlockSpec(memory_space=pltpu.VMEM),
        scratch_shapes=[
            pltpu.VMEM(table.shape, jnp.float32),
            pltpu.VMEM((total, width), jnp.float32),
        ],
        compiler_params=pltpu.CompilerParams(vmem_limit_bytes=40 * 2**20),
        name="fetch_rows",
    )(keys, table)


def patch_kernel(unroll, source_ref, place_ref, real_ref, imag_ref, rows_ref, out_ref, straight, turned, made):
    wide = rows_ref[...].astype(jnp.float32)
    straight[...] = wide
    lane = lax.broadcasted_iota(jnp.int32, wide.shape, 1)
    swapped = pltpu.roll(wide, HALF, 1)
    turned[...] = jnp.where(lane < HALF, -swapped, swapped)
    made[...] = jnp.zeros_like(made)

    def body(i, carry):
        for u in range(unroll):
            n = i * unroll + u
            row = pl.ds(source_ref[n], 1)
            made[pl.ds(place_ref[n], 1), :] = (
                real_ref[n] * straight[row, :] + imag_ref[n] * turned[row, :]
            )
        return carry

    lax.fori_loop(0, source_ref.shape[0] // unroll, body, 0)
    out_ref[...] = made[...].astype(jnp.bfloat16)


def place_patches(source, place, visibility, rows, slots):
    width = rows.shape[1]
    smem = pl.BlockSpec(memory_space=pltpu.SMEM)
    vmem = pl.BlockSpec(memory_space=pltpu.VMEM)
    return pl.pallas_call(
        functools.partial(patch_kernel, 16),
        out_shape=jax.ShapeDtypeStruct((slots, width), jnp.bfloat16),
        in_specs=[smem, smem, smem, smem, vmem],
        out_specs=vmem,
        scratch_shapes=[
            pltpu.VMEM(rows.shape, jnp.float32),
            pltpu.VMEM(rows.shape, jnp.float32),
            pltpu.VMEM((slots, width), jnp.float32),
        ],
        compiler_params=pltpu.CompilerParams(vmem_limit_bytes=40 * 2**20),
        name="place_patches",
    )(source, place, visibility[:, 0], visibility[:, 1], rows)


def paint_kernel(
    unroll, cells_ref, band_ref, patches_ref, own_ref, own_edge_ref, other_ref, other_edge_ref, wide, *canvases
):
    source = lax.broadcasted_iota(jnp.int32, (LANES, LANES), 0)
    target = lax.broadcasted_iota(jnp.int32, (LANES, LANES), 1)
    picks = [
        ((source == target + s * SUP) & (target % HALF < SUP)).astype(jnp.bfloat16) for s in range(SUP)
    ]

    def open_out(i, carry):
        first = pl.multiple_of(i * LANES, LANES)
        part = patches_ref[pl.ds(first, LANES), :]
        for s in range(SUP):
            wide[pl.ds(first * SUP + s, LANES, stride=SUP), :] = jnp.dot(
                part, picks[s], preferred_element_type=jnp.float32
            )
        return carry

    lax.fori_loop(0, patches_ref.shape[0] // LANES, open_out, 0)

    def clear(i, carry):
        start = pl.multiple_of(i * HEIGHT, SUP)
        for canvas in canvases:
            canvas[pl.ds(start, HEIGHT), :] = jnp.zeros((HEIGHT, LANES), jnp.float32)
        return carry

    lax.fori_loop(0, TILES, clear, 0)

    lane = lax.broadcasted_iota(jnp.int32, (SUP, LANES), 1)

    def body(i, carry):
        spread = []
        for u in range(unroll):
            n = i * unroll + u
            cell = cells_ref[n]
            patch = wide[pl.ds(pl.multiple_of(n * SUP, SUP), SUP), :]
            spread.append((cell >> SHIFT, pltpu.roll(patch, cell & (STRIDE - 1), 1)))
        for u, (start, moved) in enumerate(spread):
            canvas = canvases[u % len(canvases)]
            canvas[pl.ds(start, SUP), :] = canvas[pl.ds(start, SUP), :] + moved
        return carry

    lax.fori_loop(0, patches_ref.shape[0] // unroll, body, 0)

    per_block = LANES // STRIDE
    blocks = NV // LANES // 2
    lower = lane < HALF
    quarter = (lane % HALF) < STRIDE
    middle = (lane >= STRIDE) & (lane < LANES - STRIDE)

    def merge(start_block, main_ref, edge_ref):
        def column(b, carry):
            first = (start_block + b) * per_block
            at = pl.ds(pl.multiple_of(b * LANES, LANES), LANES)
            for p in range(HEIGHT // SUP):
                tiles = []
                for t in range(per_block + 1):
                    where = pl.ds(pl.multiple_of((first + t) * HEIGHT + p * SUP, SUP), SUP)
                    tile = canvases[0][where, :]
                    for canvas in canvases[1:]:
                        tile = tile + canvas[where, :]
                    tiles.append(tile)
                before, t0, t1, t2, t3 = tiles
                edges = jnp.where(quarter, t3, before)
                real = jnp.where(lower, t0, pltpu.roll(t2, HALF, 1)) + jnp.where(
                    middle, pltpu.roll(t1, STRIDE, 1), pltpu.roll(edges, LANES - STRIDE, 1)
                )
                imag = jnp.where(lower, pltpu.roll(t0, HALF, 1), t2) + jnp.where(
                    middle, pltpu.roll(t1, LANES - STRIDE, 1), pltpu.roll(edges, STRIDE, 1)
                )
                if p < ROWS // SUP:
                    rows = slice(p * SUP, (p + 1) * SUP)
                    main_ref[0, rows, at] = real
                    main_ref[1, rows, at] = imag
                else:
                    edge_ref[0, :, at] = real
                    edge_ref[1, :, at] = imag
            return carry

        lax.fori_loop(0, blocks, column, 0)

    band = band_ref[0]
    merge(band * blocks, own_ref, own_edge_ref)
    merge((1 - band) * blocks, other_ref, other_edge_ref)


def paint(cells, band, patches):
    main = jax.ShapeDtypeStruct((2, ROWS, NV // 2), jnp.float32)
    edge = jax.ShapeDtypeStruct((2, SUP, NV // 2), jnp.float32)
    smem = pl.BlockSpec(memory_space=pltpu.SMEM)
    vmem = pl.BlockSpec(memory_space=pltpu.VMEM)
    return pl.pallas_call(
        functools.partial(paint_kernel, 16),
        out_shape=(main, edge, main, edge),
        in_specs=[smem, smem, vmem],
        out_specs=(vmem, vmem, vmem, vmem),
        scratch_shapes=[pltpu.VMEM((patches.shape[0] * SUP, LANES), jnp.float32)]
        + [pltpu.VMEM((TILES * HEIGHT, LANES), jnp.float32)] * CHAINS,
        compiler_params=pltpu.CompilerParams(vmem_limit_bytes=56 * 2**20),
        name="paint",
    )(cells, band, patches)


def local(
    visibility,
    plane_index,
    beam_index,
    strip_index,
    cell_row,
    cell_column,
    phase_index,
    kernel_table,
):
    blocks = visibility.shape[0]
    strips = lax.axis_size("tile")
    planes_band, beam_count, phase_local, row_width = kernel_table.shape
    phases = phase_local * strips
    band_index = lax.axis_index("wband")
    strip_capacity = 2 * blocks // strips
    phase_capacity = 2 * blocks // phases * phase_local
    both = phase_capacity + strip_capacity

    owner = phase_index // phase_local
    key = ((plane_index - band_index * planes_band) * beam_count + beam_index) * phase_local
    key = key + phase_index % phase_local
    cell = ((cell_column // STRIDE + 1) * HEIGHT + cell_row) * STRIDE + cell_column % STRIDE

    owner_rank = rank_in_bucket(owner, strips)
    strip_rank = rank_in_bucket(strip_index, strips)
    notes = (
        jnp.zeros((strips * both,), jnp.int32)
        .at[
            jnp.concatenate(
                [owner * both + owner_rank, strip_index * both + phase_capacity + strip_rank]
            )
        ]
        .set(jnp.concatenate([key, cell]), unique_indices=True, mode="drop")
    )
    notes = lax.all_to_all(
        notes.reshape(strips, both), "tile", split_axis=0, concat_axis=0, tiled=True
    )
    keys = notes[:, :phase_capacity].reshape(-1)
    cells = notes[:, phase_capacity:].reshape(-1)

    rows = fetch_rows(keys, kernel_table.reshape(-1, row_width))
    rows = lax.all_to_all(
        rows.reshape(strips, phase_capacity, row_width), "tile", split_axis=0, concat_axis=0, tiled=True
    ).reshape(-1, row_width)
    patches = place_patches(
        owner * phase_capacity + owner_rank,
        strip_index * strip_capacity + strip_rank,
        visibility,
        rows,
        strips * strip_capacity,
    )
    patches = lax.all_to_all(
        patches.reshape(strips, strip_capacity, row_width), "tile", split_axis=0, concat_axis=0, tiled=True
    ).reshape(-1, row_width)

    own, own_edge, other, other_edge = paint(cells, band_index.reshape(1).astype(jnp.int32), patches)
    bands = lax.axis_size("wband")
    received = lax.ppermute(other, "wband", [(b, 1 - b) for b in range(bands)])
    straight = lax.ppermute(own_edge, "tile", [(t, t + 1) for t in range(strips - 1)])
    crossed = lax.ppermute(
        other_edge,
        ("wband", "tile"),
        [(b * strips + t, (1 - b) * strips + t + 1) for b in range(bands) for t in range(strips - 1)],
    )
    edge = jnp.pad(straight + crossed, ((0, 0), (0, ROWS - SUP), (0, 0)))
    return own + received + edge


def solution(mesh):
    placed = (
        P(("groups", "wband", "tile"), None),
        P(("groups", "wband", "tile")),
        P(("groups", "wband", "tile")),
        P(("groups", "wband", "tile")),
        P(("groups", "wband", "tile")),
        P(("groups", "wband", "tile")),
        P(("groups", "wband", "tile")),
        P("wband", None, "tile", None),
    )
    return jax.shard_map(
        local,
        mesh=mesh,
        in_specs=placed,
        out_specs=P(None, ("groups", "tile"), "wband"),
        check_vma=False,
    )
```

```python
import functools

import jax
import jax.numpy as jnp
from jax import lax
from jax.experimental import pallas as pl
from jax.experimental.pallas import tpu as pltpu
from jax.sharding import PartitionSpec as P

SUP = 8
NV = 8192
ROWS = 64
LANES = 128
HALF = LANES // 2
SHIFT = 5
STRIDE = 1 << SHIFT
HEIGHT = ROWS + SUP
TILES = NV // STRIDE + 1
CHAINS = 2


def rank_in_bucket(target, buckets):
    rows = target.shape[0]
    bucket = lax.broadcasted_iota(jnp.int32, (buckets, rows, LANES), 0)
    member = jnp.where(target[None] == bucket, 1.0, 0.0).reshape(buckets * rows, LANES)
    member = member.astype(jnp.bfloat16)
    up = lax.broadcasted_iota(jnp.int32, (LANES, LANES), 0)
    down = lax.broadcasted_iota(jnp.int32, (LANES, LANES), 1)
    within = jnp.dot(
        member, jnp.where(up < down, 1.0, 0.0).astype(jnp.bfloat16), preferred_element_type=jnp.float32
    )
    totals = jnp.dot(
        member, jnp.ones((LANES, LANES), jnp.bfloat16), preferred_element_type=jnp.float32
    )
    count = buckets * rows
    left = lax.broadcasted_iota(jnp.int32, (count, count), 0)
    right = lax.broadcasted_iota(jnp.int32, (count, count), 1)
    earlier = jnp.where((right < left) & (right // rows == left // rows), 1.0, 0.0)
    above = jnp.dot(
        earlier.astype(jnp.bfloat16), totals.astype(jnp.bfloat16), preferred_element_type=jnp.float32
    )
    ranks = member.astype(jnp.float32) * (within + above)
    return jnp.sum(ranks.reshape(buckets, rows, LANES), axis=0).astype(jnp.int32)


def address_kernel(
    sizes, band_ref, plane_ref, beam_ref, strip_ref, row_ref, column_ref, phase_ref,
    key_ref, cell_ref, source_ref, place_ref, key_at_ref, cell_at_ref,
):
    strips, planes_band, beam_count, phase_local, phase_capacity, strip_capacity = sizes
    both = phase_capacity + strip_capacity
    phase, strip, column = phase_ref[...], strip_ref[...], column_ref[...]
    owner = phase // phase_local
    key = ((plane_ref[...] - band_ref[0] * planes_band) * beam_count + beam_ref[...]) * phase_local
    key_ref[...] = key + (phase - owner * phase_local)
    tile_row = ((column >> SHIFT) + 1) * HEIGHT + row_ref[...]
    cell_ref[...] = tile_row * STRIDE + (column & (STRIDE - 1))
    owner_rank = rank_in_bucket(owner, strips)
    strip_rank = rank_in_bucket(strip, strips)
    source_ref[...] = owner * phase_capacity + owner_rank
    place_ref[...] = strip * strip_capacity + strip_rank
    key_at_ref[...] = owner * both + owner_rank
    cell_at_ref[...] = strip * both + phase_capacity + strip_rank


def addresses(sizes, band, *columns):
    blocks = columns[0].shape[0]
    shape = jax.ShapeDtypeStruct((blocks // LANES, LANES), jnp.int32)
    vmem = pl.BlockSpec(memory_space=pltpu.VMEM)
    results = pl.pallas_call(
        functools.partial(address_kernel, sizes),
        out_shape=(shape,) * 6,
        in_specs=[pl.BlockSpec(memory_space=pltpu.SMEM)] + [vmem] * len(columns),
        out_specs=(vmem,) * 6,
        compiler_params=pltpu.CompilerParams(vmem_limit_bytes=40 * 2**20),
        name="addresses",
    )(band, *(column.reshape(shape.shape) for column in columns))
    return [result.reshape(blocks) for result in results]


def notes_kernel(unroll, key_ref, cell_ref, key_at_ref, cell_at_ref, blank_ref, out_ref, sem):
    copy = pltpu.make_async_copy(blank_ref, out_ref, sem)
    copy.start()
    copy.wait()

    def body(i, carry):
        for u in range(unroll):
            n = i * unroll + u
            out_ref[key_at_ref[n]] = key_ref[n]
            out_ref[cell_at_ref[n]] = cell_ref[n]
        return carry

    lax.fori_loop(0, key_ref.shape[0] // unroll, body, 0)


def write_notes(key, cell, key_at, cell_at, total):
    smem = pl.BlockSpec(memory_space=pltpu.SMEM)
    return pl.pallas_call(
        functools.partial(notes_kernel, 16),
        out_shape=jax.ShapeDtypeStruct((total,), jnp.int32),
        in_specs=[smem] * 4 + [pl.BlockSpec(memory_space=pl.ANY)],
        out_specs=smem,
        scratch_shapes=[pltpu.SemaphoreType.DMA],
        name="write_notes",
    )(key, cell, key_at, cell_at, jnp.zeros((total,), jnp.int32))


def fetch_kernel(unroll, keys_ref, table_ref, out_ref, wide, picked):
    wide[...] = table_ref[...].astype(jnp.float32)

    def body(i, carry):
        for u in range(unroll):
            n = i * unroll + u
            picked[pl.ds(n, 1), :] = wide[pl.ds(keys_ref[n], 1), :]
        return carry

    lax.fori_loop(0, out_ref.shape[0] // unroll, body, 0)
    out_ref[...] = picked[...].astype(jnp.bfloat16)


def fetch_rows(keys, table):
    total, width = keys.shape[0], table.shape[1]
    return pl.pallas_call(
        functools.partial(fetch_kernel, 16),
        out_shape=jax.ShapeDtypeStruct((total, width), jnp.bfloat16),
        in_specs=[
            pl.BlockSpec(memory_space=pltpu.SMEM),
            pl.BlockSpec(memory_space=pltpu.VMEM),
        ],
        out_specs=pl.BlockSpec(memory_space=pltpu.VMEM),
        scratch_shapes=[
            pltpu.VMEM(table.shape, jnp.float32),
            pltpu.VMEM((total, width), jnp.float32),
        ],
        compiler_params=pltpu.CompilerParams(vmem_limit_bytes=40 * 2**20),
        name="fetch_rows",
    )(keys, table)


def patch_kernel(unroll, source_ref, place_ref, real_ref, imag_ref, rows_ref, out_ref, straight, turned, made):
    wide = rows_ref[...].astype(jnp.float32)
    straight[...] = wide
    lane = lax.broadcasted_iota(jnp.int32, wide.shape, 1)
    swapped = pltpu.roll(wide, HALF, 1)
    turned[...] = jnp.where(lane < HALF, -swapped, swapped)
    made[...] = jnp.zeros_like(made)

    def body(i, carry):
        for u in range(unroll):
            n = i * unroll + u
            row = pl.ds(source_ref[n], 1)
            made[pl.ds(place_ref[n], 1), :] = (
                real_ref[n] * straight[row, :] + imag_ref[n] * turned[row, :]
            )
        return carry

    lax.fori_loop(0, source_ref.shape[0] // unroll, body, 0)
    out_ref[...] = made[...].astype(jnp.bfloat16)


def place_patches(source, place, visibility, rows, slots):
    width = rows.shape[1]
    smem = pl.BlockSpec(memory_space=pltpu.SMEM)
    vmem = pl.BlockSpec(memory_space=pltpu.VMEM)
    return pl.pallas_call(
        functools.partial(patch_kernel, 16),
        out_shape=jax.ShapeDtypeStruct((slots, width), jnp.bfloat16),
        in_specs=[smem, smem, smem, smem, vmem],
        out_specs=vmem,
        scratch_shapes=[
            pltpu.VMEM(rows.shape, jnp.float32),
            pltpu.VMEM(rows.shape, jnp.float32),
            pltpu.VMEM((slots, width), jnp.float32),
        ],
        compiler_params=pltpu.CompilerParams(vmem_limit_bytes=40 * 2**20),
        name="place_patches",
    )(source, place, visibility[:, 0], visibility[:, 1], rows)


def paint_kernel(
    unroll, cells_ref, band_ref, patches_ref, own_ref, own_edge_ref, other_ref, other_edge_ref, wide, *canvases
):
    source = lax.broadcasted_iota(jnp.int32, (LANES, LANES), 0)
    target = lax.broadcasted_iota(jnp.int32, (LANES, LANES), 1)
    picks = [
        ((source == target + s * SUP) & (target % HALF < SUP)).astype(jnp.bfloat16) for s in range(SUP)
    ]

    def open_out(i, carry):
        first = pl.multiple_of(i * LANES, LANES)
        part = patches_ref[pl.ds(first, LANES), :]
        for s in range(SUP):
            wide[pl.ds(first * SUP + s, LANES, stride=SUP), :] = jnp.dot(
                part, picks[s], preferred_element_type=jnp.float32
            )
        return carry

    lax.fori_loop(0, patches_ref.shape[0] // LANES, open_out, 0)

    def clear(i, carry):
        start = pl.multiple_of(i * HEIGHT, SUP)
        for canvas in canvases:
            canvas[pl.ds(start, HEIGHT), :] = jnp.zeros((HEIGHT, LANES), jnp.float32)
        return carry

    lax.fori_loop(0, TILES, clear, 0)

    lane = lax.broadcasted_iota(jnp.int32, (SUP, LANES), 1)

    def moved_group(i):
        spread = []
        for u in range(unroll):
            n = i * unroll + u
            patch = wide[pl.ds(pl.multiple_of(n * SUP, SUP), SUP), :]
            spread.append(pltpu.roll(patch, cells_ref[n] & (STRIDE - 1), 1))
        return tuple(spread)

    def add_group(i, spread):
        for u, moved in enumerate(spread):
            start = cells_ref[i * unroll + u] >> SHIFT
            canvas = canvases[u % len(canvases)]
            canvas[pl.ds(start, SUP), :] = canvas[pl.ds(start, SUP), :] + moved

    def body(i, spread):
        following = moved_group(i + 1)
        add_group(i, spread)
        return following

    groups = patches_ref.shape[0] // unroll
    last = lax.fori_loop(0, groups - 1, body, moved_group(0))
    add_group(groups - 1, last)

    per_block = LANES // STRIDE
    blocks = NV // LANES // 2
    lower = lane < HALF
    quarter = (lane % HALF) < STRIDE
    middle = (lane >= STRIDE) & (lane < LANES - STRIDE)

    def merge(start_block, main_ref, edge_ref):
        def column(b, carry):
            first = (start_block + b) * per_block
            at = pl.ds(pl.multiple_of(b * LANES, LANES), LANES)
            for p in range(HEIGHT // SUP):
                tiles = []
                for t in range(per_block + 1):
                    where = pl.ds(pl.multiple_of((first + t) * HEIGHT + p * SUP, SUP), SUP)
                    tile = canvases[0][where, :]
                    for canvas in canvases[1:]:
                        tile = tile + canvas[where, :]
                    tiles.append(tile)
                before, t0, t1, t2, t3 = tiles
                edges = jnp.where(quarter, t3, before)
                real = jnp.where(lower, t0, pltpu.roll(t2, HALF, 1)) + jnp.where(
                    middle, pltpu.roll(t1, STRIDE, 1), pltpu.roll(edges, LANES - STRIDE, 1)
                )
                imag = jnp.where(lower, pltpu.roll(t0, HALF, 1), t2) + jnp.where(
                    middle, pltpu.roll(t1, LANES - STRIDE, 1), pltpu.roll(edges, STRIDE, 1)
                )
                if p < ROWS // SUP:
                    rows = slice(p * SUP, (p + 1) * SUP)
                    main_ref[0, rows, at] = real
                    main_ref[1, rows, at] = imag
                else:
                    edge_ref[0, :, at] = real
                    edge_ref[1, :, at] = imag
            return carry

        lax.fori_loop(0, blocks, column, 0)

    band = band_ref[0]
    merge(band * blocks, own_ref, own_edge_ref)
    merge((1 - band) * blocks, other_ref, other_edge_ref)


def paint(cells, band, patches):
    main = jax.ShapeDtypeStruct((2, ROWS, NV // 2), jnp.float32)
    edge = jax.ShapeDtypeStruct((2, SUP, NV // 2), jnp.float32)
    smem = pl.BlockSpec(memory_space=pltpu.SMEM)
    vmem = pl.BlockSpec(memory_space=pltpu.VMEM)
    return pl.pallas_call(
        functools.partial(paint_kernel, 64),
        out_shape=(main, edge, main, edge),
        in_specs=[smem, smem, vmem],
        out_specs=(vmem, vmem, vmem, vmem),
        scratch_shapes=[pltpu.VMEM((patches.shape[0] * SUP, LANES), jnp.float32)]
        + [pltpu.VMEM((TILES * HEIGHT, LANES), jnp.float32)] * CHAINS,
        compiler_params=pltpu.CompilerParams(vmem_limit_bytes=56 * 2**20),
        name="paint",
    )(cells, band, patches)


def local(
    visibility,
    plane_index,
    beam_index,
    strip_index,
    cell_row,
    cell_column,
    phase_index,
    kernel_table,
):
    blocks = visibility.shape[0]
    strips = lax.axis_size("tile")
    planes_band, beam_count, phase_local, row_width = kernel_table.shape
    phases = phase_local * strips
    band_index = lax.axis_index("wband")
    strip_capacity = 2 * blocks // strips
    phase_capacity = 2 * blocks // phases * phase_local
    both = phase_capacity + strip_capacity

    band = band_index.reshape(1).astype(jnp.int32)
    sizes = (strips, planes_band, beam_count, phase_local, phase_capacity, strip_capacity)
    key, cell, source, place, key_at, cell_at = addresses(
        sizes, band, plane_index, beam_index, strip_index, cell_row, cell_column, phase_index
    )
    notes = write_notes(key, cell, key_at, cell_at, strips * both)
    notes = lax.all_to_all(
        notes.reshape(strips, both), "tile", split_axis=0, concat_axis=0, tiled=True
    )
    keys = notes[:, :phase_capacity].reshape(-1)
    cells = notes[:, phase_capacity:].reshape(-1)

    rows = fetch_rows(keys, kernel_table.reshape(-1, row_width))
    rows = lax.all_to_all(
        rows.reshape(strips, phase_capacity, row_width), "tile", split_axis=0, concat_axis=0, tiled=True
    ).reshape(-1, row_width)
    patches = place_patches(
        source,
        place,
        visibility,
        rows,
        strips * strip_capacity,
    )
    patches = lax.all_to_all(
        patches.reshape(strips, strip_capacity, row_width), "tile", split_axis=0, concat_axis=0, tiled=True
    ).reshape(-1, row_width)

    own, own_edge, other, other_edge = paint(cells, band, patches)
    bands = lax.axis_size("wband")
    received = lax.ppermute(other, "wband", [(b, 1 - b) for b in range(bands)])
    straight = lax.ppermute(own_edge, "tile", [(t, t + 1) for t in range(strips - 1)])
    crossed = lax.ppermute(
        other_edge,
        ("wband", "tile"),
        [(b * strips + t, (1 - b) * strips + t + 1) for b in range(bands) for t in range(strips - 1)],
    )
    edge = jnp.pad(straight + crossed, ((0, 0), (0, ROWS - SUP), (0, 0)))
    return own + received + edge


def solution(mesh):
    placed = (
        P(("groups", "wband", "tile"), None),
        P(("groups", "wband", "tile")),
        P(("groups", "wband", "tile")),
        P(("groups", "wband", "tile")),
        P(("groups", "wband", "tile")),
        P(("groups", "wband", "tile")),
        P(("groups", "wband", "tile")),
        P("wband", None, "tile", None),
    )
    return jax.shard_map(
        local,
        mesh=mesh,
        in_specs=placed,
        out_specs=P(None, ("groups", "tile"), "wband"),
        check_vma=False,
    )
```

```python
import functools

import jax
import jax.numpy as jnp
from jax import lax
from jax.experimental import pallas as pl
from jax.experimental.pallas import tpu as pltpu
from jax.sharding import PartitionSpec as P

SUP = 8
NV = 8192
ROWS = 64
LANES = 128
HALF = LANES // 2
SHIFT = 5
STRIDE = 1 << SHIFT
HEIGHT = ROWS + SUP
TILES = NV // STRIDE + 1
CHAINS = 2
MESH = pl.DeviceIdType.MESH


def rank_in_bucket(target, buckets):
    rows = target.shape[0]
    bucket = lax.broadcasted_iota(jnp.int32, (buckets, rows, LANES), 0)
    member = jnp.where(target[None] == bucket, 1.0, 0.0).reshape(buckets * rows, LANES)
    member = member.astype(jnp.bfloat16)
    up = lax.broadcasted_iota(jnp.int32, (LANES, LANES), 0)
    down = lax.broadcasted_iota(jnp.int32, (LANES, LANES), 1)
    within = jnp.dot(
        member, jnp.where(up < down, 1.0, 0.0).astype(jnp.bfloat16), preferred_element_type=jnp.float32
    )
    totals = jnp.dot(
        member, jnp.ones((LANES, LANES), jnp.bfloat16), preferred_element_type=jnp.float32
    )
    count = buckets * rows
    left = lax.broadcasted_iota(jnp.int32, (count, count), 0)
    right = lax.broadcasted_iota(jnp.int32, (count, count), 1)
    earlier = jnp.where((right < left) & (right // rows == left // rows), 1.0, 0.0)
    above = jnp.dot(
        earlier.astype(jnp.bfloat16), totals.astype(jnp.bfloat16), preferred_element_type=jnp.float32
    )
    ranks = member.astype(jnp.float32) * (within + above)
    return jnp.sum(ranks.reshape(buckets, rows, LANES), axis=0).astype(jnp.int32)


def address_kernel(
    sizes, band_ref, plane_ref, beam_ref, strip_ref, row_ref, column_ref, phase_ref,
    key_ref, cell_ref, source_ref, place_ref, key_at_ref, cell_at_ref,
):
    strips, planes_band, beam_count, phase_local, phase_capacity, strip_capacity = sizes
    both = phase_capacity + strip_capacity
    phase, strip, column = phase_ref[...], strip_ref[...], column_ref[...]
    owner = phase // phase_local
    key = ((plane_ref[...] - band_ref[0] * planes_band) * beam_count + beam_ref[...]) * phase_local
    key_ref[...] = key + (phase - owner * phase_local)
    tile_row = ((column >> SHIFT) + 1) * HEIGHT + row_ref[...]
    cell_ref[...] = tile_row * STRIDE + (column & (STRIDE - 1))
    owner_rank = rank_in_bucket(owner, strips)
    strip_rank = rank_in_bucket(strip, strips)
    source_ref[...] = owner * phase_capacity + owner_rank
    place_ref[...] = strip * strip_capacity + strip_rank
    key_at_ref[...] = owner * both + owner_rank
    cell_at_ref[...] = strip * both + phase_capacity + strip_rank


def addresses(sizes, band, *columns):
    blocks = columns[0].shape[0]
    shape = jax.ShapeDtypeStruct((blocks // LANES, LANES), jnp.int32)
    vmem = pl.BlockSpec(memory_space=pltpu.VMEM)
    results = pl.pallas_call(
        functools.partial(address_kernel, sizes),
        out_shape=(shape,) * 6,
        in_specs=[pl.BlockSpec(memory_space=pltpu.SMEM)] + [vmem] * len(columns),
        out_specs=(vmem,) * 6,
        compiler_params=pltpu.CompilerParams(vmem_limit_bytes=40 * 2**20),
        name="addresses",
    )(band, *(column.reshape(shape.shape) for column in columns))
    return [result.reshape(blocks) for result in results]


def notes_kernel(unroll, key_ref, cell_ref, key_at_ref, cell_at_ref, blank_ref, out_ref, sem):
    copy = pltpu.make_async_copy(blank_ref, out_ref, sem)
    copy.start()
    copy.wait()

    def body(i, carry):
        for u in range(unroll):
            n = i * unroll + u
            out_ref[key_at_ref[n]] = key_ref[n]
            out_ref[cell_at_ref[n]] = cell_ref[n]
        return carry

    lax.fori_loop(0, key_ref.shape[0] // unroll, body, 0)


def write_notes(key, cell, key_at, cell_at, total):
    smem = pl.BlockSpec(memory_space=pltpu.SMEM)
    return pl.pallas_call(
        functools.partial(notes_kernel, 16),
        out_shape=jax.ShapeDtypeStruct((total,), jnp.int32),
        in_specs=[smem] * 4 + [pl.BlockSpec(memory_space=pl.ANY)],
        out_specs=smem,
        scratch_shapes=[pltpu.SemaphoreType.DMA],
        name="write_notes",
    )(key, cell, key_at, cell_at, jnp.zeros((total,), jnp.int32))


def peer(me, step, count):
    return lax.rem(me + step + count, count)


def greet(devices):
    barrier = pltpu.get_barrier_semaphore()
    for device in devices:
        pl.semaphore_signal(barrier, inc=1, device_id=device, device_id_type=MESH)
    return barrier


def greet_tiles(me, tiles):
    barrier = pltpu.get_barrier_semaphore()

    def body(step, carry):
        pl.semaphore_signal(
            barrier, inc=1, device_id={"tile": peer(me, step, tiles)}, device_id_type=MESH
        )
        return carry

    lax.fori_loop(1, tiles, body, 0)
    return barrier


def answer_kernel(
    tiles, capacity, unroll, notes_ref, table_ref, got_ref, rows_ref,
    wide, picked, outgoing, listed, note_send, note_recv, row_send, row_recv, own_sem,
):
    me = lax.axis_index("tile")
    barrier = greet_tiles(me, tiles)
    wide[...] = table_ref[...].astype(jnp.float32)
    pl.semaphore_wait(barrier, tiles - 1)

    def note_copy(step, sender):
        target = peer(me, step, tiles)
        return pltpu.make_async_remote_copy(
            src_ref=notes_ref.at[target],
            dst_ref=got_ref.at[sender],
            send_sem=note_send.at[step],
            recv_sem=note_recv.at[step],
            device_id={"tile": target},
            device_id_type=MESH,
        )

    def row_copy(step, sender):
        target = peer(me, step, tiles)
        return pltpu.make_async_remote_copy(
            src_ref=outgoing.at[target],
            dst_ref=rows_ref.at[sender],
            send_sem=row_send.at[step],
            recv_sem=row_recv.at[step],
            device_id={"tile": target},
            device_id_type=MESH,
        )

    def start_notes(step, carry):
        note_copy(step, me).start()
        return carry

    def wait_notes(step, carry):
        note_copy(step, peer(me, -step, tiles)).wait_recv()
        return carry

    lax.fori_loop(1, tiles, start_notes, 0)
    got_ref[me] = notes_ref[me]
    lax.fori_loop(1, tiles, wait_notes, 0)
    listing = pltpu.make_async_copy(got_ref, listed, own_sem)
    listing.start()
    listing.wait()

    def look_up(target):
        def body(i, carry):
            for u in range(unroll):
                j = i * unroll + u
                key = listed[target, j // LANES, j % LANES]
                picked[pl.ds(j, 1), :] = wide[pl.ds(key, 1), :]
            return carry

        lax.fori_loop(0, capacity // unroll, body, 0)
        outgoing[target] = picked[...].astype(jnp.bfloat16)

    def send_rows(step, carry):
        look_up(peer(me, step, tiles))
        row_copy(step, me).start()
        return carry

    lax.fori_loop(1, tiles, send_rows, 0)
    look_up(me)
    keep = pltpu.make_async_copy(outgoing.at[me], rows_ref.at[me], own_sem)
    keep.start()

    def finish(step, carry):
        sender = peer(me, -step, tiles)
        note_copy(step, sender).wait_send()
        row_copy(step, sender).wait()
        return carry

    lax.fori_loop(1, tiles, finish, 0)
    keep.wait()


def answer_requests(notes, table, tiles, capacity):
    width = table.shape[1]
    notes = notes.reshape(tiles, -1, LANES)
    vmem = pl.BlockSpec(memory_space=pltpu.VMEM)
    return pl.pallas_call(
        functools.partial(answer_kernel, tiles, capacity, 16),
        out_shape=(
            jax.ShapeDtypeStruct(notes.shape, jnp.int32),
            jax.ShapeDtypeStruct((tiles, capacity, width), jnp.bfloat16),
        ),
        in_specs=[vmem, vmem],
        out_specs=(vmem, pl.BlockSpec(memory_space=pl.ANY)),
        scratch_shapes=[
            pltpu.VMEM(table.shape, jnp.float32),
            pltpu.VMEM((capacity, width), jnp.float32),
            pltpu.VMEM((tiles, capacity, width), jnp.bfloat16),
            pltpu.SMEM(notes.shape, jnp.int32),
            pltpu.SemaphoreType.DMA((tiles,)),
            pltpu.SemaphoreType.DMA((tiles,)),
            pltpu.SemaphoreType.DMA((tiles,)),
            pltpu.SemaphoreType.DMA((tiles,)),
            pltpu.SemaphoreType.DMA,
        ],
        compiler_params=pltpu.CompilerParams(
            collective_id=0, has_side_effects=True, vmem_limit_bytes=40 * 2**20
        ),
        name="answer_requests",
    )(notes, table)


def edges_kernel(
    tiles, pieces, other_ref, own_edge_ref, other_edge_ref, got_ref, straight_ref, crossed_ref, sends, recvs
):
    me, band = lax.axis_index("tile"), lax.axis_index("wband")
    after, before = peer(me, 1, tiles), peer(me, -1, tiles)
    partner = {"wband": 1 - band}
    barrier = greet(
        [partner]
        + [{"wband": side, "tile": tile} for side in (band, 1 - band) for tile in (after, before)]
    )
    pl.semaphore_wait(barrier, 5)
    routes = [(own_edge_ref, straight_ref, {"tile": after})]
    routes.append((other_edge_ref, crossed_ref, {"wband": 1 - band, "tile": after}))
    rows = ROWS // pieces
    for component in range(2):
        for piece in range(pieces):
            part = (component, pl.ds(piece * rows, rows))
            routes.append((other_ref.at[part], got_ref.at[part], partner))
    copies = [
        pltpu.make_async_remote_copy(
            src_ref=source,
            dst_ref=target,
            send_sem=sends.at[n],
            recv_sem=recvs.at[n],
            device_id=device,
            device_id_type=MESH,
        )
        for n, (source, target, device) in enumerate(routes)
    ]
    for copy in copies:
        copy.start()
    for copy in copies:
        copy.wait()


def exchange_edges(tiles, other, own_edge, other_edge):
    hbm = pl.BlockSpec(memory_space=pl.ANY)
    pieces = 2
    count = 2 + 2 * pieces
    return pl.pallas_call(
        functools.partial(edges_kernel, tiles, pieces),
        out_shape=tuple(
            jax.ShapeDtypeStruct(x.shape, x.dtype) for x in (other, own_edge, other_edge)
        ),
        in_specs=[hbm] * 3,
        out_specs=(hbm,) * 3,
        scratch_shapes=[pltpu.SemaphoreType.DMA((count,)), pltpu.SemaphoreType.DMA((count,))],
        compiler_params=pltpu.CompilerParams(collective_id=1, has_side_effects=True),
        name="exchange_edges",
    )(other, own_edge, other_edge)


def patch_kernel(unroll, source_ref, place_ref, real_ref, imag_ref, rows_ref, out_ref, straight, turned, made):
    wide = rows_ref[...].astype(jnp.float32)
    straight[...] = wide
    lane = lax.broadcasted_iota(jnp.int32, wide.shape, 1)
    swapped = pltpu.roll(wide, HALF, 1)
    turned[...] = jnp.where(lane < HALF, -swapped, swapped)
    made[...] = jnp.zeros_like(made)

    def body(i, carry):
        for u in range(unroll):
            n = i * unroll + u
            row = pl.ds(source_ref[n], 1)
            made[pl.ds(place_ref[n], 1), :] = (
                real_ref[n] * straight[row, :] + imag_ref[n] * turned[row, :]
            )
        return carry

    lax.fori_loop(0, source_ref.shape[0] // unroll, body, 0)
    out_ref[...] = made[...].astype(jnp.bfloat16)


def place_patches(source, place, visibility, rows, slots):
    width = rows.shape[1]
    smem = pl.BlockSpec(memory_space=pltpu.SMEM)
    vmem = pl.BlockSpec(memory_space=pltpu.VMEM)
    return pl.pallas_call(
        functools.partial(patch_kernel, 16),
        out_shape=jax.ShapeDtypeStruct((slots, width), jnp.bfloat16),
        in_specs=[smem, smem, smem, smem, vmem],
        out_specs=vmem,
        scratch_shapes=[
            pltpu.VMEM(rows.shape, jnp.float32),
            pltpu.VMEM(rows.shape, jnp.float32),
            pltpu.VMEM((slots, width), jnp.float32),
        ],
        compiler_params=pltpu.CompilerParams(vmem_limit_bytes=40 * 2**20),
        name="place_patches",
    )(source, place, visibility[:, 0], visibility[:, 1], rows)


def paint_kernel(
    unroll, cells_ref, band_ref, patches_ref, own_ref, own_edge_ref, other_ref, other_edge_ref, wide, *canvases
):
    source = lax.broadcasted_iota(jnp.int32, (LANES, LANES), 0)
    target = lax.broadcasted_iota(jnp.int32, (LANES, LANES), 1)
    picks = [
        ((source == target + s * SUP) & (target % HALF < SUP)).astype(jnp.bfloat16) for s in range(SUP)
    ]

    def open_out(i, carry):
        first = pl.multiple_of(i * LANES, LANES)
        part = patches_ref[pl.ds(first, LANES), :]
        for s in range(SUP):
            wide[pl.ds(first * SUP + s, LANES, stride=SUP), :] = jnp.dot(
                part, picks[s], preferred_element_type=jnp.float32
            )
        return carry

    lax.fori_loop(0, patches_ref.shape[0] // LANES, open_out, 0)

    def clear(i, carry):
        start = pl.multiple_of(i * HEIGHT, SUP)
        for canvas in canvases:
            canvas[pl.ds(start, HEIGHT), :] = jnp.zeros((HEIGHT, LANES), jnp.float32)
        return carry

    lax.fori_loop(0, TILES, clear, 0)

    lane = lax.broadcasted_iota(jnp.int32, (SUP, LANES), 1)

    def moved_group(i):
        spread = []
        for u in range(unroll):
            n = i * unroll + u
            patch = wide[pl.ds(pl.multiple_of(n * SUP, SUP), SUP), :]
            spread.append(pltpu.roll(patch, cells_ref[n] & (STRIDE - 1), 1))
        return tuple(spread)

    def add_group(i, spread):
        for u, moved in enumerate(spread):
            start = cells_ref[i * unroll + u] >> SHIFT
            canvas = canvases[u % len(canvases)]
            canvas[pl.ds(start, SUP), :] = canvas[pl.ds(start, SUP), :] + moved

    def body(i, spread):
        following = moved_group(i + 1)
        add_group(i, spread)
        return following

    groups = patches_ref.shape[0] // unroll
    last = lax.fori_loop(0, groups - 1, body, moved_group(0))
    add_group(groups - 1, last)

    per_block = LANES // STRIDE
    blocks = NV // LANES // 2
    lower = lane < HALF
    quarter = (lane % HALF) < STRIDE
    middle = (lane >= STRIDE) & (lane < LANES - STRIDE)

    def merge(start_block, main_ref, edge_ref):
        def column(b, carry):
            first = (start_block + b) * per_block
            at = pl.ds(pl.multiple_of(b * LANES, LANES), LANES)
            for p in range(HEIGHT // SUP):
                tiles = []
                for t in range(per_block + 1):
                    where = pl.ds(pl.multiple_of((first + t) * HEIGHT + p * SUP, SUP), SUP)
                    tile = canvases[0][where, :]
                    for canvas in canvases[1:]:
                        tile = tile + canvas[where, :]
                    tiles.append(tile)
                before, t0, t1, t2, t3 = tiles
                edges = jnp.where(quarter, t3, before)
                real = jnp.where(lower, t0, pltpu.roll(t2, HALF, 1)) + jnp.where(
                    middle, pltpu.roll(t1, STRIDE, 1), pltpu.roll(edges, LANES - STRIDE, 1)
                )
                imag = jnp.where(lower, pltpu.roll(t0, HALF, 1), t2) + jnp.where(
                    middle, pltpu.roll(t1, LANES - STRIDE, 1), pltpu.roll(edges, STRIDE, 1)
                )
                if p < ROWS // SUP:
                    rows = slice(p * SUP, (p + 1) * SUP)
                    main_ref[0, rows, at] = real
                    main_ref[1, rows, at] = imag
                else:
                    edge_ref[0, :, at] = real
                    edge_ref[1, :, at] = imag
            return carry

        lax.fori_loop(0, blocks, column, 0)

    band = band_ref[0]
    merge(band * blocks, own_ref, own_edge_ref)
    merge((1 - band) * blocks, other_ref, other_edge_ref)


def paint(cells, band, patches):
    main = jax.ShapeDtypeStruct((2, ROWS, NV // 2), jnp.float32)
    edge = jax.ShapeDtypeStruct((2, SUP, NV // 2), jnp.float32)
    smem = pl.BlockSpec(memory_space=pltpu.SMEM)
    vmem = pl.BlockSpec(memory_space=pltpu.VMEM)
    return pl.pallas_call(
        functools.partial(paint_kernel, 64),
        out_shape=(main, edge, main, edge),
        in_specs=[smem, smem, vmem],
        out_specs=(vmem, vmem, vmem, vmem),
        scratch_shapes=[pltpu.VMEM((patches.shape[0] * SUP, LANES), jnp.float32)]
        + [pltpu.VMEM((TILES * HEIGHT, LANES), jnp.float32)] * CHAINS,
        compiler_params=pltpu.CompilerParams(vmem_limit_bytes=56 * 2**20),
        name="paint",
    )(cells, band, patches)


def local(
    visibility,
    plane_index,
    beam_index,
    strip_index,
    cell_row,
    cell_column,
    phase_index,
    kernel_table,
):
    blocks = visibility.shape[0]
    strips = lax.axis_size("tile")
    planes_band, beam_count, phase_local, row_width = kernel_table.shape
    phases = phase_local * strips
    band_index = lax.axis_index("wband")
    strip_capacity = 2 * blocks // strips
    phase_capacity = 2 * blocks // phases * phase_local
    both = phase_capacity + strip_capacity

    band = band_index.reshape(1).astype(jnp.int32)
    sizes = (strips, planes_band, beam_count, phase_local, phase_capacity, strip_capacity)
    key, cell, source, place, key_at, cell_at = addresses(
        sizes, band, plane_index, beam_index, strip_index, cell_row, cell_column, phase_index
    )
    notes = write_notes(key, cell, key_at, cell_at, strips * both)
    got, rows = answer_requests(
        notes, kernel_table.reshape(-1, row_width), strips, phase_capacity
    )
    cells = got.reshape(strips, both)[:, phase_capacity:].reshape(-1)
    rows = rows.reshape(-1, row_width)
    patches = place_patches(
        source,
        place,
        visibility,
        rows,
        strips * strip_capacity,
    )
    patches = lax.all_to_all(
        patches.reshape(strips, strip_capacity, row_width), "tile", split_axis=0, concat_axis=0, tiled=True
    ).reshape(-1, row_width)

    own, own_edge, other, other_edge = paint(cells, band, patches)
    received, straight, crossed = exchange_edges(strips, other, own_edge, other_edge)
    edge = jnp.where(lax.axis_index("tile") > 0, straight + crossed, 0.0)
    edge = jnp.pad(edge, ((0, 0), (0, ROWS - SUP), (0, 0)))
    return own + received + edge


def solution(mesh):
    placed = (
        P(("groups", "wband", "tile"), None),
        P(("groups", "wband", "tile")),
        P(("groups", "wband", "tile")),
        P(("groups", "wband", "tile")),
        P(("groups", "wband", "tile")),
        P(("groups", "wband", "tile")),
        P(("groups", "wband", "tile")),
        P("wband", None, "tile", None),
    )
    return jax.shard_map(
        local,
        mesh=mesh,
        in_specs=placed,
        out_specs=P(None, ("groups", "tile"), "wband"),
        check_vma=False,
    )
```

```python
import functools

import jax
import jax.numpy as jnp
from jax import lax
from jax.experimental import pallas as pl
from jax.experimental.pallas import tpu as pltpu
from jax.sharding import PartitionSpec as P

SUP = 8
NV = 8192
ROWS = 64
LANES = 128
HALF = LANES // 2
SHIFT = 5
STRIDE = 1 << SHIFT
HEIGHT = ROWS + SUP
TILES = NV // STRIDE + 1
CHAINS = 2
MESH = pl.DeviceIdType.MESH


def rank_in_bucket(target, buckets):
    rows = target.shape[0]
    bucket = lax.broadcasted_iota(jnp.int32, (buckets, rows, LANES), 0)
    member = jnp.where(target[None] == bucket, 1.0, 0.0).reshape(buckets * rows, LANES)
    member = member.astype(jnp.bfloat16)
    up = lax.broadcasted_iota(jnp.int32, (LANES, LANES), 0)
    down = lax.broadcasted_iota(jnp.int32, (LANES, LANES), 1)
    within = jnp.dot(
        member, jnp.where(up < down, 1.0, 0.0).astype(jnp.bfloat16), preferred_element_type=jnp.float32
    )
    totals = jnp.dot(
        member, jnp.ones((LANES, LANES), jnp.bfloat16), preferred_element_type=jnp.float32
    )
    count = buckets * rows
    left = lax.broadcasted_iota(jnp.int32, (count, count), 0)
    right = lax.broadcasted_iota(jnp.int32, (count, count), 1)
    earlier = jnp.where((right < left) & (right // rows == left // rows), 1.0, 0.0)
    above = jnp.dot(
        earlier.astype(jnp.bfloat16), totals.astype(jnp.bfloat16), preferred_element_type=jnp.float32
    )
    ranks = member.astype(jnp.float32) * (within + above)
    return jnp.sum(ranks.reshape(buckets, rows, LANES), axis=0).astype(jnp.int32)


def spread_to_slots(position, total, *pieces):
    high_count = total // LANES
    high, low = position // LANES, position % LANES
    high_slot = lax.broadcasted_iota(jnp.int32, (high_count, LANES), 0)
    low_slot = lax.broadcasted_iota(jnp.int32, (LANES, LANES), 0)
    sums = jnp.zeros((len(pieces) * high_count, LANES), jnp.float32)
    for a in range(position.shape[0]):
        at_high = high[a : a + 1] == high_slot
        values = [jnp.where(at_high, piece[a : a + 1], 0.0) for piece in pieces]
        left = jnp.concatenate(values, axis=0).astype(jnp.bfloat16)
        right = jnp.where(low[a : a + 1] == low_slot, 1.0, 0.0).astype(jnp.bfloat16)
        sums = sums + lax.dot_general(
            left, right, (((1,), (1,)), ((), ())), preferred_element_type=jnp.float32
        )
    return [sums[i * high_count : (i + 1) * high_count] for i in range(len(pieces))]


def bytes_of(values):
    return [((values >> shift) & 255).astype(jnp.float32) for shift in (16, 8, 0)]


def from_bytes(top, middle, bottom):
    return (top * 65536.0 + middle * 256.0 + bottom).astype(jnp.int32)


def thirds_of(values):
    top = values.astype(jnp.bfloat16).astype(jnp.float32)
    rest = values - top
    middle = rest.astype(jnp.bfloat16).astype(jnp.float32)
    return [top, middle, rest - middle]


def address_kernel(
    sizes, band_ref, plane_ref, beam_ref, strip_ref, row_ref, column_ref, phase_ref, real_ref, imag_ref,
    notes_ref, source_ref, slot_real_ref, slot_imag_ref,
):
    strips, planes_band, beam_count, phase_local, phase_capacity, strip_capacity = sizes
    both = phase_capacity + strip_capacity
    phase, strip, column = phase_ref[...], strip_ref[...], column_ref[...]
    owner = phase // phase_local
    key = ((plane_ref[...] - band_ref[0] * planes_band) * beam_count + beam_ref[...]) * phase_local
    key = key + (phase - owner * phase_local)
    tile_row = ((column >> SHIFT) + 1) * HEIGHT + row_ref[...]
    cell = tile_row * STRIDE + (column & (STRIDE - 1))
    owner_rank = rank_in_bucket(owner, strips)
    strip_rank = rank_in_bucket(strip, strips)
    total = strips * both
    keys = spread_to_slots(owner * both + owner_rank, total, *bytes_of(key))
    cells = spread_to_slots(strip * both + phase_capacity + strip_rank, total, *bytes_of(cell))
    notes_ref[...] = from_bytes(*(k + c for k, c in zip(keys, cells)))
    slots = spread_to_slots(
        strip * strip_capacity + strip_rank,
        strips * strip_capacity,
        *bytes_of(owner * phase_capacity + owner_rank),
        *thirds_of(real_ref[...]),
        *thirds_of(imag_ref[...]),
    )
    source_ref[...] = from_bytes(*slots[:3])
    slot_real_ref[...] = slots[3] + slots[4] + slots[5]
    slot_imag_ref[...] = slots[6] + slots[7] + slots[8]


def addresses(sizes, band, *columns):
    strips, _, _, _, phase_capacity, strip_capacity = sizes
    blocks = columns[0].shape[0]
    slots = strips * strip_capacity
    vmem = pl.BlockSpec(memory_space=pltpu.VMEM)

    def shape(count, kind):
        return jax.ShapeDtypeStruct((count // LANES, LANES), kind)

    return pl.pallas_call(
        functools.partial(address_kernel, sizes),
        out_shape=(
            shape(strips * phase_capacity + slots, jnp.int32),
            shape(slots, jnp.int32),
            shape(slots, jnp.float32),
            shape(slots, jnp.float32),
        ),
        in_specs=[pl.BlockSpec(memory_space=pltpu.SMEM)] + [vmem] * len(columns),
        out_specs=(vmem,) * 4,
        compiler_params=pltpu.CompilerParams(vmem_limit_bytes=40 * 2**20),
        name="addresses",
    )(band, *(column.reshape(blocks // LANES, LANES) for column in columns))


def peer(me, step, count):
    return lax.rem(me + step + count, count)


def greet(devices):
    barrier = pltpu.get_barrier_semaphore()
    for device in devices:
        pl.semaphore_signal(barrier, inc=1, device_id=device, device_id_type=MESH)
    return barrier


def greet_tiles(me, tiles):
    barrier = pltpu.get_barrier_semaphore()

    def body(step, carry):
        pl.semaphore_signal(
            barrier, inc=1, device_id={"tile": peer(me, step, tiles)}, device_id_type=MESH
        )
        return carry

    lax.fori_loop(1, tiles, body, 0)
    return barrier


def far_first(k, tiles):
    up, down = tiles // 2 + k // 2, tiles // 2 - (k + 1) // 2
    return jnp.where(k % 2 == 0, up, down)


def answer_kernel(
    tiles, capacity, unroll, notes_ref, table_ref, got_ref, rows_ref,
    wide, picked, outgoing, listed, note_send, note_recv, row_send, row_recv, own_sem,
):
    me = lax.axis_index("tile")
    barrier = greet_tiles(me, tiles)
    wide[...] = table_ref[...].astype(jnp.float32)
    pl.semaphore_wait(barrier, tiles - 1)

    def note_copy(step, sender):
        target = peer(me, step, tiles)
        return pltpu.make_async_remote_copy(
            src_ref=notes_ref.at[target],
            dst_ref=got_ref.at[sender],
            send_sem=note_send.at[step],
            recv_sem=note_recv.at[step],
            device_id={"tile": target},
            device_id_type=MESH,
        )

    def row_copy(step, sender):
        target = peer(me, step, tiles)
        return pltpu.make_async_remote_copy(
            src_ref=outgoing.at[target],
            dst_ref=rows_ref.at[sender],
            send_sem=row_send.at[step],
            recv_sem=row_recv.at[step],
            device_id={"tile": target},
            device_id_type=MESH,
        )

    def start_notes(step, carry):
        note_copy(step, me).start()
        return carry

    def wait_notes(step, carry):
        note_copy(step, peer(me, -step, tiles)).wait_recv()
        return carry

    lax.fori_loop(1, tiles, start_notes, 0)
    got_ref[me] = notes_ref[me]
    lax.fori_loop(1, tiles, wait_notes, 0)
    listing = pltpu.make_async_copy(got_ref, listed, own_sem)
    listing.start()
    listing.wait()

    def look_up(target):
        def body(i, carry):
            for u in range(unroll):
                j = i * unroll + u
                key = listed[target, j // LANES, j % LANES]
                picked[pl.ds(j, 1), :] = wide[pl.ds(key, 1), :]
            return carry

        lax.fori_loop(0, capacity // unroll, body, 0)
        outgoing[target] = picked[...].astype(jnp.bfloat16)

    def send_rows(k, carry):
        step = far_first(k, tiles)
        look_up(peer(me, step, tiles))
        row_copy(step, me).start()
        return carry

    lax.fori_loop(0, tiles - 1, send_rows, 0)
    look_up(me)
    keep = pltpu.make_async_copy(outgoing.at[me], rows_ref.at[me], own_sem)
    keep.start()

    def finish(step, carry):
        sender = peer(me, -step, tiles)
        note_copy(step, sender).wait_send()
        row_copy(step, sender).wait()
        return carry

    lax.fori_loop(1, tiles, finish, 0)
    keep.wait()


def answer_requests(notes, table, tiles, capacity):
    width = table.shape[1]
    notes = notes.reshape(tiles, -1, LANES)
    vmem = pl.BlockSpec(memory_space=pltpu.VMEM)
    return pl.pallas_call(
        functools.partial(answer_kernel, tiles, capacity, 16),
        out_shape=(
            jax.ShapeDtypeStruct(notes.shape, jnp.int32),
            jax.ShapeDtypeStruct((tiles, capacity, width), jnp.bfloat16),
        ),
        in_specs=[vmem, vmem],
        out_specs=(vmem, pl.BlockSpec(memory_space=pl.ANY)),
        scratch_shapes=[
            pltpu.VMEM(table.shape, jnp.float32),
            pltpu.VMEM((capacity, width), jnp.float32),
            pltpu.VMEM((tiles, capacity, width), jnp.bfloat16),
            pltpu.SMEM(notes.shape, jnp.int32),
            pltpu.SemaphoreType.DMA((tiles,)),
            pltpu.SemaphoreType.DMA((tiles,)),
            pltpu.SemaphoreType.DMA((tiles,)),
            pltpu.SemaphoreType.DMA((tiles,)),
            pltpu.SemaphoreType.DMA,
        ],
        compiler_params=pltpu.CompilerParams(
            collective_id=0, has_side_effects=True, vmem_limit_bytes=40 * 2**20
        ),
        name="answer_requests",
    )(notes, table)


def edges_kernel(
    tiles, pieces, other_ref, own_edge_ref, other_edge_ref, got_ref, straight_ref, crossed_ref, sends, recvs
):
    me, band = lax.axis_index("tile"), lax.axis_index("wband")
    after, before = peer(me, 1, tiles), peer(me, -1, tiles)
    partner = {"wband": 1 - band}
    barrier = greet(
        [partner]
        + [{"wband": side, "tile": tile} for side in (band, 1 - band) for tile in (after, before)]
    )
    pl.semaphore_wait(barrier, 5)
    routes = [(own_edge_ref, straight_ref, {"tile": after})]
    routes.append((other_edge_ref, crossed_ref, {"wband": 1 - band, "tile": after}))
    rows = ROWS // pieces
    for component in range(2):
        for piece in range(pieces):
            part = (component, pl.ds(piece * rows, rows))
            routes.append((other_ref.at[part], got_ref.at[part], partner))
    copies = [
        pltpu.make_async_remote_copy(
            src_ref=source,
            dst_ref=target,
            send_sem=sends.at[n],
            recv_sem=recvs.at[n],
            device_id=device,
            device_id_type=MESH,
        )
        for n, (source, target, device) in enumerate(routes)
    ]
    for copy in copies:
        copy.start()
    for copy in copies:
        copy.wait()


def exchange_edges(tiles, other, own_edge, other_edge):
    hbm = pl.BlockSpec(memory_space=pl.ANY)
    pieces = 2
    count = 2 + 2 * pieces
    return pl.pallas_call(
        functools.partial(edges_kernel, tiles, pieces),
        out_shape=tuple(
            jax.ShapeDtypeStruct(x.shape, x.dtype) for x in (other, own_edge, other_edge)
        ),
        in_specs=[hbm] * 3,
        out_specs=(hbm,) * 3,
        scratch_shapes=[pltpu.SemaphoreType.DMA((count,)), pltpu.SemaphoreType.DMA((count,))],
        compiler_params=pltpu.CompilerParams(collective_id=1, has_side_effects=True),
        name="exchange_edges",
    )(other, own_edge, other_edge)


def patch_kernel(
    tiles, unroll, source_ref, real_ref, imag_ref, rows_ref, patches_ref,
    wide, real_scale, imag_scale, picked, outgoing, sends, recvs, own_sem,
):
    me = lax.axis_index("tile")
    barrier = greet_tiles(me, tiles)
    wide[...] = rows_ref[...].astype(jnp.float32)

    def scale(g, carry):
        at = pl.ds(pl.multiple_of(g * LANES, LANES), LANES)
        for values, scales in ((real_ref, real_scale), (imag_ref, imag_scale)):
            scales[at, :] = jnp.broadcast_to(values[pl.ds(g, 1), :], (LANES, LANES)).T
        return carry

    lax.fori_loop(0, real_ref.shape[0], scale, 0)
    pl.semaphore_wait(barrier, tiles - 1)
    capacity = picked.shape[0]
    lane = lax.broadcasted_iota(jnp.int32, picked.shape, 1)

    def copy(step, sender):
        target = peer(me, step, tiles)
        return pltpu.make_async_remote_copy(
            src_ref=outgoing.at[target],
            dst_ref=patches_ref.at[sender],
            send_sem=sends.at[step],
            recv_sem=recvs.at[step],
            device_id={"tile": target},
            device_id_type=MESH,
        )

    def make(target):
        def body(i, carry):
            for u in range(unroll):
                j = i * unroll + u
                picked[pl.ds(j, 1), :] = wide[pl.ds(source_ref[target * capacity + j], 1), :]
            return carry

        lax.fori_loop(0, capacity // unroll, body, 0)
        at = pl.ds(pl.multiple_of(target * capacity, capacity), capacity)
        straight = picked[...]
        swapped = pltpu.roll(straight, HALF, 1)
        turned = jnp.where(lane < HALF, -swapped, swapped)
        made = real_scale[at, :] * straight + imag_scale[at, :] * turned
        outgoing[target] = made.astype(jnp.bfloat16)

    def send(k, carry):
        step = far_first(k, tiles)
        make(peer(me, step, tiles))
        copy(step, me).start()
        return carry

    lax.fori_loop(0, tiles - 1, send, 0)
    make(me)
    keep = pltpu.make_async_copy(outgoing.at[me], patches_ref.at[me], own_sem)
    keep.start()

    def finish(step, carry):
        copy(step, peer(me, -step, tiles)).wait()
        return carry

    lax.fori_loop(1, tiles, finish, 0)
    keep.wait()


def send_patches(source, real, imag, rows, tiles):
    slots, width = real.size, rows.shape[1]
    capacity = slots // tiles
    vmem = pl.BlockSpec(memory_space=pltpu.VMEM)
    return pl.pallas_call(
        functools.partial(patch_kernel, tiles, 16),
        out_shape=jax.ShapeDtypeStruct((tiles, capacity, width), jnp.bfloat16),
        in_specs=[pl.BlockSpec(memory_space=pltpu.SMEM), vmem, vmem, vmem],
        out_specs=pl.BlockSpec(memory_space=pl.ANY),
        scratch_shapes=[
            pltpu.VMEM(rows.shape, jnp.float32),
            pltpu.VMEM((slots, width), jnp.float32),
            pltpu.VMEM((slots, width), jnp.float32),
            pltpu.VMEM((capacity, width), jnp.float32),
            pltpu.VMEM((tiles, capacity, width), jnp.bfloat16),
            pltpu.SemaphoreType.DMA((tiles,)),
            pltpu.SemaphoreType.DMA((tiles,)),
            pltpu.SemaphoreType.DMA,
        ],
        compiler_params=pltpu.CompilerParams(
            collective_id=2, has_side_effects=True, vmem_limit_bytes=40 * 2**20
        ),
        name="send_patches",
    )(source.reshape(-1), real, imag, rows)


def paint_kernel(
    unroll, cells_ref, band_ref, patches_ref, own_ref, own_edge_ref, other_ref, other_edge_ref, wide, *canvases
):
    source = lax.broadcasted_iota(jnp.int32, (LANES, LANES), 0)
    target = lax.broadcasted_iota(jnp.int32, (LANES, LANES), 1)
    picks = [
        ((source == target + s * SUP) & (target % HALF < SUP)).astype(jnp.bfloat16) for s in range(SUP)
    ]

    def open_out(i, carry):
        first = pl.multiple_of(i * LANES, LANES)
        part = patches_ref[pl.ds(first, LANES), :]
        for s in range(SUP):
            wide[pl.ds(first * SUP + s, LANES, stride=SUP), :] = jnp.dot(
                part, picks[s], preferred_element_type=jnp.float32
            )
        return carry

    lax.fori_loop(0, patches_ref.shape[0] // LANES, open_out, 0)

    def clear(i, carry):
        start = pl.multiple_of(i * HEIGHT, SUP)
        for canvas in canvases:
            canvas[pl.ds(start, HEIGHT), :] = jnp.zeros((HEIGHT, LANES), jnp.float32)
        return carry

    lax.fori_loop(0, TILES, clear, 0)

    lane = lax.broadcasted_iota(jnp.int32, (SUP, LANES), 1)

    def moved_group(i):
        spread = []
        for u in range(unroll):
            n = i * unroll + u
            patch = wide[pl.ds(pl.multiple_of(n * SUP, SUP), SUP), :]
            spread.append(pltpu.roll(patch, cells_ref[n] & (STRIDE - 1), 1))
        return tuple(spread)

    def add_group(i, spread):
        for u, moved in enumerate(spread):
            start = cells_ref[i * unroll + u] >> SHIFT
            canvas = canvases[u % len(canvases)]
            canvas[pl.ds(start, SUP), :] = canvas[pl.ds(start, SUP), :] + moved

    def body(i, spread):
        following = moved_group(i + 1)
        add_group(i, spread)
        return following

    groups = patches_ref.shape[0] // unroll
    last = lax.fori_loop(0, groups - 1, body, moved_group(0))
    add_group(groups - 1, last)

    per_block = LANES // STRIDE
    blocks = NV // LANES // 2
    lower = lane < HALF
    quarter = (lane % HALF) < STRIDE
    middle = (lane >= STRIDE) & (lane < LANES - STRIDE)

    def merge(start_block, main_ref, edge_ref):
        def column(b, carry):
            first = (start_block + b) * per_block
            at = pl.ds(pl.multiple_of(b * LANES, LANES), LANES)
            merged = []
            for p in range(HEIGHT // SUP):
                tiles = []
                for t in range(per_block + 1):
                    where = pl.ds(pl.multiple_of((first + t) * HEIGHT + p * SUP, SUP), SUP)
                    tile = canvases[0][where, :]
                    for canvas in canvases[1:]:
                        tile = tile + canvas[where, :]
                    tiles.append(tile)
                before, t0, t1, t2, t3 = tiles
                edges = jnp.where(quarter, t3, before)
                real = jnp.where(lower, t0, pltpu.roll(t2, HALF, 1)) + jnp.where(
                    middle, pltpu.roll(t1, STRIDE, 1), pltpu.roll(edges, LANES - STRIDE, 1)
                )
                imag = jnp.where(lower, pltpu.roll(t0, HALF, 1), t2) + jnp.where(
                    middle, pltpu.roll(t1, LANES - STRIDE, 1), pltpu.roll(edges, STRIDE, 1)
                )
                merged.append((real, imag))
            for p in range(0, ROWS // SUP, 2):
                rows = slice(p * SUP, (p + 2) * SUP)
                for k in range(2):
                    pair = jnp.concatenate([merged[p][k], merged[p + 1][k]], axis=0)
                    main_ref[k, rows, at] = pair.astype(main_ref.dtype)
            edge_ref[:, at] = jnp.concatenate(merged[-1], axis=0).astype(edge_ref.dtype)
            return carry

        lax.fori_loop(0, blocks, column, 0)

    band = band_ref[0]
    merge(band * blocks, own_ref, own_edge_ref)
    merge((1 - band) * blocks, other_ref, other_edge_ref)


def paint(cells, band, patches):
    main = jax.ShapeDtypeStruct((2, ROWS, NV // 2), jnp.float32)
    other = jax.ShapeDtypeStruct(main.shape, jnp.bfloat16)
    edge = jax.ShapeDtypeStruct((2 * SUP, NV // 2), jnp.bfloat16)
    smem = pl.BlockSpec(memory_space=pltpu.SMEM)
    vmem = pl.BlockSpec(memory_space=pltpu.VMEM)
    return pl.pallas_call(
        functools.partial(paint_kernel, 64),
        out_shape=(main, edge, other, edge),
        in_specs=[smem, smem, vmem],
        out_specs=(vmem, vmem, vmem, vmem),
        scratch_shapes=[pltpu.VMEM((patches.shape[0] * SUP, LANES), jnp.float32)]
        + [pltpu.VMEM((TILES * HEIGHT, LANES), jnp.float32)] * CHAINS,
        compiler_params=pltpu.CompilerParams(vmem_limit_bytes=56 * 2**20),
        name="paint",
    )(cells, band, patches)


def local(
    visibility,
    plane_index,
    beam_index,
    strip_index,
    cell_row,
    cell_column,
    phase_index,
    kernel_table,
):
    blocks = visibility.shape[0]
    strips = lax.axis_size("tile")
    planes_band, beam_count, phase_local, row_width = kernel_table.shape
    phases = phase_local * strips
    band_index = lax.axis_index("wband")
    strip_capacity = 2 * blocks // strips
    phase_capacity = 2 * blocks // phases * phase_local
    both = phase_capacity + strip_capacity

    band = band_index.reshape(1).astype(jnp.int32)
    sizes = (strips, planes_band, beam_count, phase_local, phase_capacity, strip_capacity)
    notes, source, slot_real, slot_imag = addresses(
        sizes, band, plane_index, beam_index, strip_index, cell_row, cell_column, phase_index,
        visibility[:, 0], visibility[:, 1],
    )
    got, rows = answer_requests(
        notes, kernel_table.reshape(-1, row_width), strips, phase_capacity
    )
    cells = got.reshape(strips, both)[:, phase_capacity:].reshape(-1)
    patches = send_patches(source, slot_real, slot_imag, rows.reshape(-1, row_width), strips)
    patches = patches.reshape(-1, row_width)

    own, own_edge, other, other_edge = paint(cells, band, patches)
    received, straight, crossed = exchange_edges(strips, other, own_edge, other_edge)
    edge = straight.astype(jnp.float32) + crossed.astype(jnp.float32)
    edge = jnp.where(lax.axis_index("tile") > 0, edge, 0.0).reshape(2, SUP, -1)
    edge = jnp.pad(edge, ((0, 0), (0, ROWS - SUP), (0, 0)))
    return own + received.astype(jnp.float32) + edge


def solution(mesh):
    placed = (
        P(("groups", "wband", "tile"), None),
        P(("groups", "wband", "tile")),
        P(("groups", "wband", "tile")),
        P(("groups", "wband", "tile")),
        P(("groups", "wband", "tile")),
        P(("groups", "wband", "tile")),
        P(("groups", "wband", "tile")),
        P("wband", None, "tile", None),
    )
    return jax.shard_map(
        local,
        mesh=mesh,
        in_specs=placed,
        out_specs=P(None, ("groups", "tile"), "wband"),
        check_vma=False,
    )
```

```python
import functools
import math

import jax
import jax.numpy as jnp
from jax import lax
from jax.experimental import pallas as pl
from jax.experimental.pallas import tpu as pltpu
from jax.sharding import PartitionSpec as P

SUP = 8
NV = 8192
ROWS = 64
LANES = 128
HALF = LANES // 2
SHIFT = 5
STRIDE = 1 << SHIFT
HEIGHT = ROWS + SUP
TILES = NV // STRIDE + 1
CHAINS = 2
MESH = pl.DeviceIdType.MESH


def rank_in_bucket(target, buckets):
    rows = target.shape[0]
    bucket = lax.broadcasted_iota(jnp.int32, (buckets, rows, LANES), 0)
    member = jnp.where(target[None] == bucket, 1.0, 0.0).reshape(buckets * rows, LANES)
    member = member.astype(jnp.bfloat16)
    up = lax.broadcasted_iota(jnp.int32, (LANES, LANES), 0)
    down = lax.broadcasted_iota(jnp.int32, (LANES, LANES), 1)
    within = jnp.dot(
        member, jnp.where(up < down, 1.0, 0.0).astype(jnp.bfloat16), preferred_element_type=jnp.float32
    )
    totals = jnp.dot(
        member, jnp.ones((LANES, LANES), jnp.bfloat16), preferred_element_type=jnp.float32
    )
    count = buckets * rows
    left = lax.broadcasted_iota(jnp.int32, (count, count), 0)
    right = lax.broadcasted_iota(jnp.int32, (count, count), 1)
    earlier = jnp.where((right < left) & (right // rows == left // rows), 1.0, 0.0)
    above = jnp.dot(
        earlier.astype(jnp.bfloat16), totals.astype(jnp.bfloat16), preferred_element_type=jnp.float32
    )
    ranks = member.astype(jnp.float32) * (within + above)
    return jnp.sum(ranks.reshape(buckets, rows, LANES), axis=0).astype(jnp.int32)


def spread_to_slots(position, total, *pieces):
    high_count = total // LANES
    high, low = position // LANES, position % LANES
    high_slot = lax.broadcasted_iota(jnp.int32, (high_count, LANES), 0)
    low_slot = lax.broadcasted_iota(jnp.int32, (LANES, LANES), 0)
    sums = jnp.zeros((len(pieces) * high_count, LANES), jnp.float32)
    for a in range(position.shape[0]):
        at_high = high[a : a + 1] == high_slot
        values = [jnp.where(at_high, piece[a : a + 1], 0.0) for piece in pieces]
        left = jnp.concatenate(values, axis=0).astype(jnp.bfloat16)
        right = jnp.where(low[a : a + 1] == low_slot, 1.0, 0.0).astype(jnp.bfloat16)
        sums = sums + lax.dot_general(
            left, right, (((1,), (1,)), ((), ())), preferred_element_type=jnp.float32
        )
    return [sums[i * high_count : (i + 1) * high_count] for i in range(len(pieces))]


def bytes_of(values):
    return [((values >> shift) & 255).astype(jnp.float32) for shift in (16, 8, 0)]


def from_bytes(top, middle, bottom):
    return (top * 65536.0 + middle * 256.0 + bottom).astype(jnp.int32)


def thirds_of(values):
    top = values.astype(jnp.bfloat16).astype(jnp.float32)
    rest = values - top
    middle = rest.astype(jnp.bfloat16).astype(jnp.float32)
    return [top, middle, rest - middle]


def address_kernel(
    sizes, band_ref, plane_ref, beam_ref, strip_ref, row_ref, column_ref, phase_ref, real_ref, imag_ref,
    notes_ref, source_ref, slot_real_ref, slot_imag_ref,
):
    strips, planes_band, beam_count, phase_local, phase_capacity, strip_capacity = sizes
    both = phase_capacity + strip_capacity
    phase, strip, column = phase_ref[...], strip_ref[...], column_ref[...]
    owner = phase // phase_local
    key = ((plane_ref[...] - band_ref[0] * planes_band) * beam_count + beam_ref[...]) * phase_local
    key = key + (phase - owner * phase_local)
    tile_row = ((column >> SHIFT) + 1) * HEIGHT + row_ref[...]
    cell = tile_row * STRIDE + (column & (STRIDE - 1))
    owner_rank = rank_in_bucket(owner, strips)
    strip_rank = rank_in_bucket(strip, strips)
    total = strips * both
    keys = spread_to_slots(owner * both + owner_rank, total, *bytes_of(key))
    cells = spread_to_slots(strip * both + phase_capacity + strip_rank, total, *bytes_of(cell))
    notes_ref[...] = from_bytes(*(k + c for k, c in zip(keys, cells)))
    slots = spread_to_slots(
        strip * strip_capacity + strip_rank,
        strips * strip_capacity,
        *bytes_of(owner * phase_capacity + owner_rank),
        *thirds_of(real_ref[...]),
        *thirds_of(imag_ref[...]),
    )
    source_ref[...] = from_bytes(*slots[:3])
    slot_real_ref[...] = slots[3] + slots[4] + slots[5]
    slot_imag_ref[...] = slots[6] + slots[7] + slots[8]


def addresses(sizes, band, *columns):
    strips, _, _, _, phase_capacity, strip_capacity = sizes
    blocks = columns[0].shape[0]
    slots = strips * strip_capacity
    vmem = pl.BlockSpec(memory_space=pltpu.VMEM)

    def shape(count, kind):
        return jax.ShapeDtypeStruct((count // LANES, LANES), kind)

    return pl.pallas_call(
        functools.partial(address_kernel, sizes),
        out_shape=(
            shape(strips * phase_capacity + slots, jnp.int32),
            shape(slots, jnp.int32),
            shape(slots, jnp.float32),
            shape(slots, jnp.float32),
        ),
        in_specs=[pl.BlockSpec(memory_space=pltpu.SMEM)] + [vmem] * len(columns),
        out_specs=(vmem,) * 4,
        compiler_params=pltpu.CompilerParams(vmem_limit_bytes=40 * 2**20),
        name="addresses",
    )(band, *(column.reshape(blocks // LANES, LANES) for column in columns))


def peer(me, step, count):
    return lax.rem(me + step + count, count)


def greet(devices):
    barrier = pltpu.get_barrier_semaphore()
    for device in devices:
        pl.semaphore_signal(barrier, inc=1, device_id=device, device_id_type=MESH)
    return barrier


def greet_tiles(me, tiles):
    barrier = pltpu.get_barrier_semaphore()

    def body(step, carry):
        pl.semaphore_signal(
            barrier, inc=1, device_id={"tile": peer(me, step, tiles)}, device_id_type=MESH
        )
        return carry

    lax.fori_loop(1, tiles, body, 0)
    return barrier


def far_first(k, tiles):
    up, down = tiles // 2 + k // 2, tiles // 2 - (k + 1) // 2
    return jnp.where(k % 2 == 0, up, down)


def trade_kernel(
    tiles, phase_capacity, strip_capacity, unroll,
    source_ref, notes_ref, table_ref, real_ref, imag_ref, got_ref, patches_ref,
    table, wide, picked, outgoing, incoming, straight, real_scale, imag_scale, chosen, leaving, listed,
    note_send, note_recv, row_send, row_recv, patch_send, patch_recv, table_sem, own_sem,
):
    me = lax.axis_index("tile")
    barrier = greet_tiles(me, tiles)
    fetch_table = pltpu.make_async_copy(table_ref, table, table_sem)
    fetch_table.start()
    pl.semaphore_wait(barrier, tiles - 1)

    def copier(source, target_ref, sends, recvs):
        def copy(step, sender):
            target = peer(me, step, tiles)
            return pltpu.make_async_remote_copy(
                src_ref=source.at[target],
                dst_ref=target_ref.at[sender],
                send_sem=sends.at[step],
                recv_sem=recvs.at[step],
                device_id={"tile": target},
                device_id_type=MESH,
            )

        return copy

    note_copy = copier(notes_ref, got_ref, note_send, note_recv)
    row_copy = copier(outgoing, incoming, row_send, row_recv)
    patch_copy = copier(leaving, patches_ref, patch_send, patch_recv)

    def start_notes(step, carry):
        note_copy(step, me).start()
        return carry

    def wait_notes(step, carry):
        note_copy(step, peer(me, -step, tiles)).wait_recv()
        return carry

    lax.fori_loop(1, tiles, start_notes, 0)
    got_ref[me] = notes_ref[me]
    fetch_table.wait()
    wide[...] = table[...].astype(jnp.float32)
    lax.fori_loop(1, tiles, wait_notes, 0)
    listing = pltpu.make_async_copy(got_ref, listed, own_sem)
    listing.start()
    listing.wait()
    groups = LANES // unroll
    group_shift = groups.bit_length() - 1

    def look_up(target):
        def body(i, carry):
            line, lane = i >> group_shift, (i & (groups - 1)) * unroll
            for u in range(unroll):
                key = listed[target, line, lane + u]
                picked[pl.ds(i * unroll + u, 1), :] = wide[pl.ds(key, 1), :]
            return carry

        lax.fori_loop(0, phase_capacity // unroll, body, 0)
        return picked[...]

    def send_rows(k, carry):
        step = far_first(k, tiles)
        target = peer(me, step, tiles)
        outgoing[target] = look_up(target).astype(jnp.bfloat16)
        row_copy(step, me).start()
        return carry

    lax.fori_loop(0, tiles - 1, send_rows, 0)

    def rows_of(tile):
        return pl.ds(pl.multiple_of(tile * phase_capacity, phase_capacity), phase_capacity)

    straight[rows_of(me), :] = look_up(me)

    def scale(g, carry):
        at = pl.ds(pl.multiple_of(g * LANES, LANES), LANES)
        for values, scales in ((real_ref, real_scale), (imag_ref, imag_scale)):
            scales[at, :] = jnp.broadcast_to(values[pl.ds(g, 1), :], (LANES, LANES)).T
        return carry

    lax.fori_loop(0, real_ref.shape[0], scale, 0)

    def take_rows(k, carry):
        step = tiles - 1 - k
        sender = peer(me, -step, tiles)
        row_copy(step, sender).wait_recv()
        straight[rows_of(sender), :] = incoming[sender].astype(jnp.float32)
        return carry

    lax.fori_loop(0, tiles - 1, take_rows, 0)
    lane_of = lax.broadcasted_iota(jnp.int32, chosen.shape, 1)

    def make(target):
        def body(i, carry):
            for u in range(unroll):
                j = i * unroll + u
                row = source_ref[target * strip_capacity + j]
                chosen[pl.ds(j, 1), :] = straight[pl.ds(row, 1), :]
            return carry

        lax.fori_loop(0, strip_capacity // unroll, body, 0)
        at = pl.ds(pl.multiple_of(target * strip_capacity, strip_capacity), strip_capacity)
        kernel = chosen[...]
        swapped = pltpu.roll(kernel, HALF, 1)
        turned = jnp.where(lane_of < HALF, -swapped, swapped)
        made = real_scale[at, :] * kernel + imag_scale[at, :] * turned
        leaving[target] = made.astype(jnp.bfloat16)

    def send_patches(k, carry):
        step = far_first(k, tiles)
        make(peer(me, step, tiles))
        patch_copy(step, me).start()
        return carry

    lax.fori_loop(0, tiles - 1, send_patches, 0)
    make(me)
    keep = pltpu.make_async_copy(leaving.at[me], patches_ref.at[me], own_sem)
    keep.start()

    def finish(step, carry):
        sender = peer(me, -step, tiles)
        note_copy(step, sender).wait_send()
        row_copy(step, sender).wait_send()
        patch_copy(step, sender).wait()
        return carry

    lax.fori_loop(1, tiles, finish, 0)
    keep.wait()


def trade(source, notes, table, real, imag, tiles, phase_capacity, strip_capacity):
    width = table.shape[1]
    notes = notes.reshape(tiles, -1, LANES)
    vmem = pl.BlockSpec(memory_space=pltpu.VMEM)
    hbm = pl.BlockSpec(memory_space=pl.ANY)
    scales = pltpu.VMEM((tiles * strip_capacity, width), jnp.float32)
    rows = pltpu.VMEM((tiles, phase_capacity, width), jnp.bfloat16)
    each = pltpu.SemaphoreType.DMA((tiles,))
    return pl.pallas_call(
        functools.partial(trade_kernel, tiles, phase_capacity, strip_capacity, 16),
        out_shape=(
            jax.ShapeDtypeStruct(notes.shape, jnp.int32),
            jax.ShapeDtypeStruct((tiles, strip_capacity, width), jnp.bfloat16),
        ),
        in_specs=[pl.BlockSpec(memory_space=pltpu.SMEM), vmem, hbm, vmem, vmem],
        out_specs=(vmem, hbm),
        scratch_shapes=[
            pltpu.VMEM(table.shape, jnp.bfloat16),
            pltpu.VMEM(table.shape, jnp.float32),
            pltpu.VMEM((phase_capacity, width), jnp.float32),
            rows,
            rows,
            pltpu.VMEM((tiles * phase_capacity, width), jnp.float32),
            scales,
            scales,
            pltpu.VMEM((strip_capacity, width), jnp.float32),
            pltpu.VMEM((tiles, strip_capacity, width), jnp.bfloat16),
            pltpu.SMEM(notes.shape, jnp.int32),
            each, each, each, each, each, each,
            pltpu.SemaphoreType.DMA,
            pltpu.SemaphoreType.DMA,
        ],
        compiler_params=pltpu.CompilerParams(
            collective_id=0, has_side_effects=True, vmem_limit_bytes=40 * 2**20
        ),
        name="trade",
    )(source.reshape(-1), notes, table, real, imag)


def edges_kernel(
    tiles, pieces, other_ref, own_edge_ref, other_edge_ref, got_ref, straight_ref, crossed_ref, sends, recvs
):
    me, band = lax.axis_index("tile"), lax.axis_index("wband")
    after, before = peer(me, 1, tiles), peer(me, -1, tiles)
    partner = {"wband": 1 - band}
    barrier = greet(
        [partner]
        + [{"wband": side, "tile": tile} for side in (band, 1 - band) for tile in (after, before)]
    )
    pl.semaphore_wait(barrier, 5)
    routes = [(own_edge_ref, straight_ref, {"tile": after})]
    routes.append((other_edge_ref, crossed_ref, {"wband": 1 - band, "tile": after}))
    rows = ROWS // pieces
    for component in range(2):
        for piece in range(pieces):
            part = (component, pl.ds(piece * rows, rows))
            routes.append((other_ref.at[part], got_ref.at[part], partner))
    copies = [
        pltpu.make_async_remote_copy(
            src_ref=source,
            dst_ref=target,
            send_sem=sends.at[n],
            recv_sem=recvs.at[n],
            device_id=device,
            device_id_type=MESH,
        )
        for n, (source, target, device) in enumerate(routes)
    ]
    for copy in copies:
        copy.start()
    for copy in copies:
        copy.wait()


def exchange_edges(tiles, other, own_edge, other_edge):
    hbm = pl.BlockSpec(memory_space=pl.ANY)
    pieces = 2
    count = 2 + 2 * pieces
    return pl.pallas_call(
        functools.partial(edges_kernel, tiles, pieces),
        out_shape=tuple(
            jax.ShapeDtypeStruct(x.shape, x.dtype) for x in (other, own_edge, other_edge)
        ),
        in_specs=[hbm] * 3,
        out_specs=(hbm,) * 3,
        scratch_shapes=[pltpu.SemaphoreType.DMA((count,)), pltpu.SemaphoreType.DMA((count,))],
        compiler_params=pltpu.CompilerParams(collective_id=1, has_side_effects=True),
        name="exchange_edges",
    )(other, own_edge, other_edge)


def paint_kernel(
    unroll, cells_ref, band_ref, patches_ref, own_ref, own_edge_ref, other_ref, other_edge_ref, wide, *canvases
):
    source = lax.broadcasted_iota(jnp.int32, (LANES, LANES), 0)
    target = lax.broadcasted_iota(jnp.int32, (LANES, LANES), 1)
    picks = [
        ((source == target + s * SUP) & (target % HALF < SUP)).astype(jnp.bfloat16) for s in range(SUP)
    ]

    chunk = math.gcd(patches_ref.shape[0], 1024)

    def open_out(i, carry):
        first = pl.multiple_of(i * chunk, chunk)
        part = patches_ref[pl.ds(first, chunk), :]
        for s in range(SUP):
            wide[pl.ds(first * SUP + s, chunk, stride=SUP), :] = jnp.dot(
                part, picks[s], preferred_element_type=jnp.float32
            )
        return carry

    lax.fori_loop(0, patches_ref.shape[0] // chunk, open_out, 0)

    def clear(i, carry):
        start = pl.multiple_of(i * HEIGHT, SUP)
        for canvas in canvases:
            canvas[pl.ds(start, HEIGHT), :] = jnp.zeros((HEIGHT, LANES), jnp.float32)
        return carry

    lax.fori_loop(0, TILES, clear, 0)

    lane = lax.broadcasted_iota(jnp.int32, (SUP, LANES), 1)

    def moved_group(i):
        spread = []
        for u in range(unroll):
            n = i * unroll + u
            patch = wide[pl.ds(pl.multiple_of(n * SUP, SUP), SUP), :]
            spread.append(pltpu.roll(patch, cells_ref[n] & (STRIDE - 1), 1))
        return tuple(spread)

    def add_group(i, spread):
        for u, moved in enumerate(spread):
            start = cells_ref[i * unroll + u] >> SHIFT
            canvas = canvases[u % len(canvases)]
            canvas[pl.ds(start, SUP), :] = canvas[pl.ds(start, SUP), :] + moved

    def body(i, spread):
        following = moved_group(i + 1)
        add_group(i, spread)
        return following

    groups = patches_ref.shape[0] // unroll
    last = lax.fori_loop(0, groups - 1, body, moved_group(0))
    add_group(groups - 1, last)

    per_block = LANES // STRIDE
    blocks = NV // LANES // 2
    lower = lane < HALF
    quarter = (lane % HALF) < STRIDE
    middle = (lane >= STRIDE) & (lane < LANES - STRIDE)

    def merge(start_block, main_ref, edge_ref):
        def column(b, carry):
            first = (start_block + b) * per_block
            at = pl.ds(pl.multiple_of(b * LANES, LANES), LANES)
            merged = []
            for p in range(HEIGHT // SUP):
                tiles = []
                for t in range(per_block + 1):
                    where = pl.ds(pl.multiple_of((first + t) * HEIGHT + p * SUP, SUP), SUP)
                    tile = canvases[0][where, :]
                    for canvas in canvases[1:]:
                        tile = tile + canvas[where, :]
                    tiles.append(tile)
                before, t0, t1, t2, t3 = tiles
                edges = jnp.where(quarter, t3, before)
                real = jnp.where(lower, t0, pltpu.roll(t2, HALF, 1)) + jnp.where(
                    middle, pltpu.roll(t1, STRIDE, 1), pltpu.roll(edges, LANES - STRIDE, 1)
                )
                imag = jnp.where(lower, pltpu.roll(t0, HALF, 1), t2) + jnp.where(
                    middle, pltpu.roll(t1, LANES - STRIDE, 1), pltpu.roll(edges, STRIDE, 1)
                )
                merged.append((real, imag))
            for p in range(0, ROWS // SUP, 2):
                rows = slice(p * SUP, (p + 2) * SUP)
                for k in range(2):
                    pair = jnp.concatenate([merged[p][k], merged[p + 1][k]], axis=0)
                    main_ref[k, rows, at] = pair.astype(main_ref.dtype)
            edge_ref[:, at] = jnp.concatenate(merged[-1], axis=0).astype(edge_ref.dtype)
            return carry

        lax.fori_loop(0, blocks, column, 0, unroll=4)

    band = band_ref[0]
    merge(band * blocks, own_ref, own_edge_ref)
    merge((1 - band) * blocks, other_ref, other_edge_ref)


def paint(cells, band, patches):
    main = jax.ShapeDtypeStruct((2, ROWS, NV // 2), jnp.float32)
    other = jax.ShapeDtypeStruct(main.shape, jnp.bfloat16)
    edge = jax.ShapeDtypeStruct((2 * SUP, NV // 2), jnp.bfloat16)
    smem = pl.BlockSpec(memory_space=pltpu.SMEM)
    vmem = pl.BlockSpec(memory_space=pltpu.VMEM)
    return pl.pallas_call(
        functools.partial(paint_kernel, 128),
        out_shape=(main, edge, other, edge),
        in_specs=[smem, smem, vmem],
        out_specs=(vmem, vmem, vmem, vmem),
        scratch_shapes=[pltpu.VMEM((patches.shape[0] * SUP, LANES), jnp.float32)]
        + [pltpu.VMEM((TILES * HEIGHT, LANES), jnp.float32)] * CHAINS,
        compiler_params=pltpu.CompilerParams(vmem_limit_bytes=56 * 2**20),
        name="paint",
    )(cells, band, patches)


def local(
    visibility,
    plane_index,
    beam_index,
    strip_index,
    cell_row,
    cell_column,
    phase_index,
    kernel_table,
):
    blocks = visibility.shape[0]
    strips = lax.axis_size("tile")
    planes_band, beam_count, phase_local, row_width = kernel_table.shape
    phases = phase_local * strips
    band_index = lax.axis_index("wband")
    strip_capacity = 2 * blocks // strips
    phase_capacity = 2 * blocks // phases * phase_local
    both = phase_capacity + strip_capacity

    band = band_index.reshape(1).astype(jnp.int32)
    sizes = (strips, planes_band, beam_count, phase_local, phase_capacity, strip_capacity)
    notes, source, slot_real, slot_imag = addresses(
        sizes, band, plane_index, beam_index, strip_index, cell_row, cell_column, phase_index,
        visibility[:, 0], visibility[:, 1],
    )
    got, patches = trade(
        source, notes, kernel_table.reshape(-1, row_width), slot_real, slot_imag,
        strips, phase_capacity, strip_capacity,
    )
    cells = got.reshape(strips, both)[:, phase_capacity:].reshape(-1)
    patches = patches.reshape(-1, row_width)

    own, own_edge, other, other_edge = paint(cells, band, patches)
    received, straight, crossed = exchange_edges(strips, other, own_edge, other_edge)
    edge = straight.astype(jnp.float32) + crossed.astype(jnp.float32)
    edge = jnp.where(lax.axis_index("tile") > 0, edge, 0.0).reshape(2, SUP, -1)
    edge = jnp.pad(edge, ((0, 0), (0, ROWS - SUP), (0, 0)))
    return own + received.astype(jnp.float32) + edge


def solution(mesh):
    placed = (
        P(("groups", "wband", "tile"), None),
        P(("groups", "wband", "tile")),
        P(("groups", "wband", "tile")),
        P(("groups", "wband", "tile")),
        P(("groups", "wband", "tile")),
        P(("groups", "wband", "tile")),
        P(("groups", "wband", "tile")),
        P("wband", None, "tile", None),
    )
    return jax.shard_map(
        local,
        mesh=mesh,
        in_specs=placed,
        out_specs=P(None, ("groups", "tile"), "wband"),
        check_vma=False,
    )
```

```python
import functools
import math

import jax
import jax.numpy as jnp
from jax import lax
from jax.experimental import pallas as pl
from jax.experimental.pallas import tpu as pltpu
from jax.sharding import PartitionSpec as P

SUP = 8
NV = 8192
ROWS = 64
LANES = 128
HALF = LANES // 2
SHIFT = 5
STRIDE = 1 << SHIFT
HEIGHT = ROWS + SUP
TILES = NV // STRIDE + 1
CHAINS = 2
MESH = pl.DeviceIdType.MESH


def rank_in_bucket(target, buckets):
    rows = target.shape[0]
    bucket = lax.broadcasted_iota(jnp.int32, (buckets, rows, LANES), 0)
    member = jnp.where(target[None] == bucket, 1.0, 0.0).reshape(buckets * rows, LANES)
    member = member.astype(jnp.bfloat16)
    up = lax.broadcasted_iota(jnp.int32, (LANES, LANES), 0)
    down = lax.broadcasted_iota(jnp.int32, (LANES, LANES), 1)
    within = jnp.dot(
        member, jnp.where(up < down, 1.0, 0.0).astype(jnp.bfloat16), preferred_element_type=jnp.float32
    )
    totals = jnp.dot(
        member, jnp.ones((LANES, LANES), jnp.bfloat16), preferred_element_type=jnp.float32
    )
    count = buckets * rows
    left = lax.broadcasted_iota(jnp.int32, (count, count), 0)
    right = lax.broadcasted_iota(jnp.int32, (count, count), 1)
    earlier = jnp.where((right < left) & (right // rows == left // rows), 1.0, 0.0)
    above = jnp.dot(
        earlier.astype(jnp.bfloat16), totals.astype(jnp.bfloat16), preferred_element_type=jnp.float32
    )
    ranks = member.astype(jnp.float32) * (within + above)
    return jnp.sum(ranks.reshape(buckets, rows, LANES), axis=0).astype(jnp.int32)


def spread_to_slots(position, total, *pieces):
    high_count = total // LANES
    high, low = position // LANES, position % LANES
    high_slot = lax.broadcasted_iota(jnp.int32, (high_count, LANES), 0)
    low_slot = lax.broadcasted_iota(jnp.int32, (LANES, LANES), 0)
    sums = jnp.zeros((len(pieces) * high_count, LANES), jnp.float32)
    for a in range(position.shape[0]):
        at_high = high[a : a + 1] == high_slot
        values = [jnp.where(at_high, piece[a : a + 1], 0.0) for piece in pieces]
        left = jnp.concatenate(values, axis=0).astype(jnp.bfloat16)
        right = jnp.where(low[a : a + 1] == low_slot, 1.0, 0.0).astype(jnp.bfloat16)
        sums = sums + lax.dot_general(
            left, right, (((1,), (1,)), ((), ())), preferred_element_type=jnp.float32
        )
    return [sums[i * high_count : (i + 1) * high_count] for i in range(len(pieces))]


def bytes_of(values):
    return [((values >> shift) & 255).astype(jnp.float32) for shift in (16, 8, 0)]


def from_bytes(top, middle, bottom):
    return (top * 65536.0 + middle * 256.0 + bottom).astype(jnp.int32)


def thirds_of(values):
    top = values.astype(jnp.bfloat16).astype(jnp.float32)
    rest = values - top
    middle = rest.astype(jnp.bfloat16).astype(jnp.float32)
    return [top, middle, rest - middle]


def address_kernel(
    sizes, band_ref, plane_ref, beam_ref, strip_ref, row_ref, column_ref, phase_ref, real_ref, imag_ref,
    notes_ref, source_ref, slot_real_ref, slot_imag_ref,
):
    strips, planes_band, beam_count, phase_local, phase_capacity, strip_capacity = sizes
    both = phase_capacity + strip_capacity
    phase, strip, column = phase_ref[...], strip_ref[...], column_ref[...]
    owner = phase // phase_local
    key = ((plane_ref[...] - band_ref[0] * planes_band) * beam_count + beam_ref[...]) * phase_local
    key = key + (phase - owner * phase_local)
    tile_row = ((column >> SHIFT) + 1) * HEIGHT + row_ref[...]
    cell = tile_row * STRIDE + (column & (STRIDE - 1))
    owner_rank = rank_in_bucket(owner, strips)
    strip_rank = rank_in_bucket(strip, strips)
    total = strips * both
    keys = spread_to_slots(owner * both + owner_rank, total, *bytes_of(key))
    cells = spread_to_slots(strip * both + phase_capacity + strip_rank, total, *bytes_of(cell))
    notes_ref[...] = from_bytes(*(k + c for k, c in zip(keys, cells)))
    slots = spread_to_slots(
        strip * strip_capacity + strip_rank,
        strips * strip_capacity,
        *bytes_of(owner * phase_capacity + owner_rank),
        *thirds_of(real_ref[...]),
        *thirds_of(imag_ref[...]),
    )
    source_ref[...] = from_bytes(*slots[:3])
    slot_real_ref[...] = slots[3] + slots[4] + slots[5]
    slot_imag_ref[...] = slots[6] + slots[7] + slots[8]


def addresses(sizes, band, *columns):
    strips, _, _, _, phase_capacity, strip_capacity = sizes
    blocks = columns[0].shape[0]
    slots = strips * strip_capacity
    vmem = pl.BlockSpec(memory_space=pltpu.VMEM)

    def shape(count, kind):
        return jax.ShapeDtypeStruct((count // LANES, LANES), kind)

    return pl.pallas_call(
        functools.partial(address_kernel, sizes),
        out_shape=(
            shape(strips * phase_capacity + slots, jnp.int32),
            shape(slots, jnp.int32),
            shape(slots, jnp.float32),
            shape(slots, jnp.float32),
        ),
        in_specs=[pl.BlockSpec(memory_space=pltpu.SMEM)] + [vmem] * len(columns),
        out_specs=(vmem,) * 4,
        compiler_params=pltpu.CompilerParams(vmem_limit_bytes=58 * 2**20),
        name="addresses",
    )(band, *(column.reshape(blocks // LANES, LANES) for column in columns))


def peer(me, step, count):
    return lax.rem(me + step + count, count)


def greet(devices):
    barrier = pltpu.get_barrier_semaphore()
    for device in devices:
        pl.semaphore_signal(barrier, inc=1, device_id=device, device_id_type=MESH)
    return barrier


def greet_tiles(me, tiles):
    barrier = pltpu.get_barrier_semaphore()

    def body(step, carry):
        pl.semaphore_signal(
            barrier, inc=1, device_id={"tile": peer(me, step, tiles)}, device_id_type=MESH
        )
        return carry

    lax.fori_loop(1, tiles, body, 0)
    return barrier


def far_first(k, tiles):
    up, down = tiles // 2 + k // 2, tiles // 2 - (k + 1) // 2
    return jnp.where(k % 2 == 0, up, down)


def trade_kernel(
    tiles, phase_capacity, strip_capacity, unroll,
    source_ref, notes_ref, table_ref, real_ref, imag_ref, got_ref, patches_ref,
    table, wide, picked, outgoing, incoming, straight, real_scale, imag_scale, chosen, leaving, listed,
    note_send, note_recv, row_send, row_recv, patch_send, patch_recv, table_sem, own_sem,
):
    me = lax.axis_index("tile")
    barrier = greet_tiles(me, tiles)
    fetch_table = pltpu.make_async_copy(table_ref, table, table_sem)
    fetch_table.start()
    pl.semaphore_wait(barrier, tiles - 1)

    def copier(source, target_ref, sends, recvs):
        def copy(step, sender):
            target = peer(me, step, tiles)
            return pltpu.make_async_remote_copy(
                src_ref=source.at[target],
                dst_ref=target_ref.at[sender],
                send_sem=sends.at[step],
                recv_sem=recvs.at[step],
                device_id={"tile": target},
                device_id_type=MESH,
            )

        return copy

    note_copy = copier(notes_ref, got_ref, note_send, note_recv)
    row_copy = copier(outgoing, incoming, row_send, row_recv)
    patch_copy = copier(leaving, patches_ref, patch_send, patch_recv)

    def start_notes(step, carry):
        note_copy(step, me).start()
        return carry

    def wait_notes(step, carry):
        note_copy(step, peer(me, -step, tiles)).wait_recv()
        return carry

    lax.fori_loop(1, tiles, start_notes, 0)
    got_ref[me] = notes_ref[me]
    fetch_table.wait()
    wide[...] = table[...].astype(jnp.float32)
    lax.fori_loop(1, tiles, wait_notes, 0)
    listing = pltpu.make_async_copy(got_ref, listed, own_sem)
    listing.start()
    listing.wait()
    groups = LANES // unroll
    group_shift = groups.bit_length() - 1

    def look_up(target):
        def body(i, carry):
            line, lane = i >> group_shift, (i & (groups - 1)) * unroll
            for u in range(unroll):
                key = listed[target, line, lane + u]
                picked[pl.ds(i * unroll + u, 1), :] = wide[pl.ds(key, 1), :]
            return carry

        lax.fori_loop(0, phase_capacity // unroll, body, 0)
        return picked[...]

    def send_rows(k, carry):
        step = far_first(k, tiles)
        target = peer(me, step, tiles)
        outgoing[target] = look_up(target).astype(jnp.bfloat16)
        row_copy(step, me).start()
        return carry

    lax.fori_loop(0, tiles - 1, send_rows, 0)

    def rows_of(tile):
        return pl.ds(pl.multiple_of(tile * phase_capacity, phase_capacity), phase_capacity)

    straight[rows_of(me), :] = look_up(me)

    def scale(g, carry):
        at = pl.ds(pl.multiple_of(g * LANES, LANES), LANES)
        for values, scales in ((real_ref, real_scale), (imag_ref, imag_scale)):
            scales[at, :] = jnp.broadcast_to(values[pl.ds(g, 1), :], (LANES, LANES)).T
        return carry

    lax.fori_loop(0, real_ref.shape[0], scale, 0)

    def take_rows(k, carry):
        step = tiles - 1 - k
        sender = peer(me, -step, tiles)
        row_copy(step, sender).wait_recv()
        straight[rows_of(sender), :] = incoming[sender].astype(jnp.float32)
        return carry

    lax.fori_loop(0, tiles - 1, take_rows, 0)
    lane_of = lax.broadcasted_iota(jnp.int32, chosen.shape, 1)

    def make(target):
        def body(i, carry):
            for u in range(unroll):
                j = i * unroll + u
                row = source_ref[target * strip_capacity + j]
                chosen[pl.ds(j, 1), :] = straight[pl.ds(row, 1), :]
            return carry

        lax.fori_loop(0, strip_capacity // unroll, body, 0)
        at = pl.ds(pl.multiple_of(target * strip_capacity, strip_capacity), strip_capacity)
        kernel = chosen[...]
        swapped = pltpu.roll(kernel, HALF, 1)
        turned = jnp.where(lane_of < HALF, -swapped, swapped)
        made = real_scale[at, :] * kernel + imag_scale[at, :] * turned
        leaving[target] = made.astype(jnp.bfloat16)

    def send_patches(k, carry):
        step = far_first(k, tiles)
        make(peer(me, step, tiles))
        patch_copy(step, me).start()
        return carry

    lax.fori_loop(0, tiles - 1, send_patches, 0)
    make(me)
    keep = pltpu.make_async_copy(leaving.at[me], patches_ref.at[me], own_sem)
    keep.start()

    def finish(step, carry):
        sender = peer(me, -step, tiles)
        note_copy(step, sender).wait_send()
        row_copy(step, sender).wait_send()
        patch_copy(step, sender).wait()
        return carry

    lax.fori_loop(1, tiles, finish, 0)
    keep.wait()


def trade(source, notes, table, real, imag, tiles, phase_capacity, strip_capacity):
    width = table.shape[1]
    notes = notes.reshape(tiles, -1, LANES)
    vmem = pl.BlockSpec(memory_space=pltpu.VMEM)
    hbm = pl.BlockSpec(memory_space=pl.ANY)
    scales = pltpu.VMEM((tiles * strip_capacity, width), jnp.float32)
    rows = pltpu.VMEM((tiles, phase_capacity, width), jnp.bfloat16)
    each = pltpu.SemaphoreType.DMA((tiles,))
    return pl.pallas_call(
        functools.partial(trade_kernel, tiles, phase_capacity, strip_capacity, 16),
        out_shape=(
            jax.ShapeDtypeStruct(notes.shape, jnp.int32),
            jax.ShapeDtypeStruct((tiles, strip_capacity, width), jnp.bfloat16),
        ),
        in_specs=[pl.BlockSpec(memory_space=pltpu.SMEM), vmem, hbm, vmem, vmem],
        out_specs=(vmem, hbm),
        scratch_shapes=[
            pltpu.VMEM(table.shape, jnp.bfloat16),
            pltpu.VMEM(table.shape, jnp.float32),
            pltpu.VMEM((phase_capacity, width), jnp.float32),
            rows,
            rows,
            pltpu.VMEM((tiles * phase_capacity, width), jnp.float32),
            scales,
            scales,
            pltpu.VMEM((strip_capacity, width), jnp.float32),
            pltpu.VMEM((tiles, strip_capacity, width), jnp.bfloat16),
            pltpu.SMEM(notes.shape, jnp.int32),
            each, each, each, each, each, each,
            pltpu.SemaphoreType.DMA,
            pltpu.SemaphoreType.DMA,
        ],
        compiler_params=pltpu.CompilerParams(
            collective_id=0, has_side_effects=True, vmem_limit_bytes=58 * 2**20
        ),
        name="trade",
    )(source.reshape(-1), notes, table, real, imag)


def edges_kernel(
    tiles, pieces, other_ref, own_edge_ref, other_edge_ref, got_ref, straight_ref, crossed_ref, sends, recvs
):
    me, band = lax.axis_index("tile"), lax.axis_index("wband")
    after, before = peer(me, 1, tiles), peer(me, -1, tiles)
    partner = {"wband": 1 - band}
    barrier = greet(
        [partner]
        + [{"wband": side, "tile": tile} for side in (band, 1 - band) for tile in (after, before)]
    )
    pl.semaphore_wait(barrier, 5)
    routes = [(own_edge_ref, straight_ref, {"tile": after})]
    routes.append((other_edge_ref, crossed_ref, {"wband": 1 - band, "tile": after}))
    rows = ROWS // pieces
    for component in range(2):
        for piece in range(pieces):
            part = (component, pl.ds(piece * rows, rows))
            routes.append((other_ref.at[part], got_ref.at[part], partner))
    copies = [
        pltpu.make_async_remote_copy(
            src_ref=source,
            dst_ref=target,
            send_sem=sends.at[n],
            recv_sem=recvs.at[n],
            device_id=device,
            device_id_type=MESH,
        )
        for n, (source, target, device) in enumerate(routes)
    ]
    for copy in copies:
        copy.start()
    for copy in copies:
        copy.wait()


def exchange_edges(tiles, other, own_edge, other_edge):
    hbm = pl.BlockSpec(memory_space=pl.ANY)
    pieces = 2
    count = 2 + 2 * pieces
    return pl.pallas_call(
        functools.partial(edges_kernel, tiles, pieces),
        out_shape=tuple(
            jax.ShapeDtypeStruct(x.shape, x.dtype) for x in (other, own_edge, other_edge)
        ),
        in_specs=[hbm] * 3,
        out_specs=(hbm,) * 3,
        scratch_shapes=[pltpu.SemaphoreType.DMA((count,)), pltpu.SemaphoreType.DMA((count,))],
        compiler_params=pltpu.CompilerParams(
            collective_id=1, has_side_effects=True, vmem_limit_bytes=58 * 2**20
        ),
        name="exchange_edges",
    )(other, own_edge, other_edge)


def paint_kernel(
    unroll, cells_ref, band_ref, patches_ref, own_ref, own_edge_ref, other_ref, other_edge_ref, wide, *canvases
):
    source = lax.broadcasted_iota(jnp.int32, (LANES, LANES), 0)
    target = lax.broadcasted_iota(jnp.int32, (LANES, LANES), 1)
    picks = [
        ((source == target + s * SUP) & (target % HALF < SUP)).astype(jnp.bfloat16) for s in range(SUP)
    ]

    chunk = math.gcd(patches_ref.shape[0], 1024)

    def open_out(i, carry):
        first = pl.multiple_of(i * chunk, chunk)
        part = patches_ref[pl.ds(first, chunk), :]
        for s in range(SUP):
            wide[pl.ds(first * SUP + s, chunk, stride=SUP), :] = jnp.dot(
                part, picks[s], preferred_element_type=jnp.float32
            )
        return carry

    lax.fori_loop(0, patches_ref.shape[0] // chunk, open_out, 0)

    def clear(i, carry):
        start = pl.multiple_of(i * HEIGHT, SUP)
        for canvas in canvases:
            canvas[pl.ds(start, HEIGHT), :] = jnp.zeros((HEIGHT, LANES), jnp.float32)
        return carry

    lax.fori_loop(0, TILES, clear, 0)

    lane = lax.broadcasted_iota(jnp.int32, (SUP, LANES), 1)

    def moved_group(i):
        spread = []
        for u in range(unroll):
            n = i * unroll + u
            patch = wide[pl.ds(pl.multiple_of(n * SUP, SUP), SUP), :]
            spread.append(pltpu.roll(patch, cells_ref[n] & (STRIDE - 1), 1))
        return tuple(spread)

    def add_group(i, spread):
        for u, moved in enumerate(spread):
            start = cells_ref[i * unroll + u] >> SHIFT
            canvas = canvases[u % len(canvases)]
            canvas[pl.ds(start, SUP), :] = canvas[pl.ds(start, SUP), :] + moved

    def body(i, spread):
        following = moved_group(i + 1)
        add_group(i, spread)
        return following

    groups = patches_ref.shape[0] // unroll
    last = lax.fori_loop(0, groups - 1, body, moved_group(0))
    add_group(groups - 1, last)

    per_block = LANES // STRIDE
    blocks = NV // LANES // 2
    lower = lane < HALF
    quarter = (lane % HALF) < STRIDE
    middle = (lane >= STRIDE) & (lane < LANES - STRIDE)

    def merge(start_block, main_ref, edge_ref):
        def column(b, carry):
            first = (start_block + b) * per_block
            at = pl.ds(pl.multiple_of(b * LANES, LANES), LANES)
            merged = []
            for p in range(HEIGHT // SUP):
                tiles = []
                for t in range(per_block + 1):
                    where = pl.ds(pl.multiple_of((first + t) * HEIGHT + p * SUP, SUP), SUP)
                    tile = canvases[0][where, :]
                    for canvas in canvases[1:]:
                        tile = tile + canvas[where, :]
                    tiles.append(tile)
                before, t0, t1, t2, t3 = tiles
                edges = jnp.where(quarter, t3, before)
                real = jnp.where(lower, t0, pltpu.roll(t2, HALF, 1)) + jnp.where(
                    middle, pltpu.roll(t1, STRIDE, 1), pltpu.roll(edges, LANES - STRIDE, 1)
                )
                imag = jnp.where(lower, pltpu.roll(t0, HALF, 1), t2) + jnp.where(
                    middle, pltpu.roll(t1, LANES - STRIDE, 1), pltpu.roll(edges, STRIDE, 1)
                )
                merged.append((real, imag))
            for p in range(0, ROWS // SUP, 2):
                rows = slice(p * SUP, (p + 2) * SUP)
                for k in range(2):
                    pair = jnp.concatenate([merged[p][k], merged[p + 1][k]], axis=0)
                    main_ref[k, rows, at] = pair.astype(main_ref.dtype)
            edge_ref[:, at] = jnp.concatenate(merged[-1], axis=0).astype(edge_ref.dtype)
            return carry

        lax.fori_loop(0, blocks, column, 0, unroll=4)

    band = band_ref[0]
    merge(band * blocks, own_ref, own_edge_ref)
    merge((1 - band) * blocks, other_ref, other_edge_ref)


def paint(cells, band, patches):
    main = jax.ShapeDtypeStruct((2, ROWS, NV // 2), jnp.float32)
    other = jax.ShapeDtypeStruct(main.shape, jnp.bfloat16)
    edge = jax.ShapeDtypeStruct((2 * SUP, NV // 2), jnp.bfloat16)
    smem = pl.BlockSpec(memory_space=pltpu.SMEM)
    vmem = pl.BlockSpec(memory_space=pltpu.VMEM)
    return pl.pallas_call(
        functools.partial(paint_kernel, 128),
        out_shape=(main, edge, other, edge),
        in_specs=[smem, smem, vmem],
        out_specs=(vmem, vmem, vmem, vmem),
        scratch_shapes=[pltpu.VMEM((patches.shape[0] * SUP, LANES), jnp.float32)]
        + [pltpu.VMEM((TILES * HEIGHT, LANES), jnp.float32)] * CHAINS,
        compiler_params=pltpu.CompilerParams(vmem_limit_bytes=56 * 2**20),
        name="paint",
    )(cells, band, patches)


def add_up_kernel(own_ref, received_ref, straight_ref, crossed_ref, out_ref):
    total = own_ref[...] + received_ref[...].astype(jnp.float32)
    edge = straight_ref[...].astype(jnp.float32) + crossed_ref[...].astype(jnp.float32)
    edge = jnp.where(lax.axis_index("tile") > 0, edge, 0.0)
    out_ref[...] = total
    for k in range(2):
        out_ref[k, :SUP, :] = total[k, :SUP] + edge[k * SUP : (k + 1) * SUP]


def add_up(own, received, straight, crossed):
    columns = 512
    full = pl.BlockSpec((2, ROWS, columns), lambda c: (0, 0, c))
    edge = pl.BlockSpec((2 * SUP, columns), lambda c: (0, c))
    return pl.pallas_call(
        add_up_kernel,
        out_shape=jax.ShapeDtypeStruct(own.shape, own.dtype),
        grid=(own.shape[2] // columns,),
        in_specs=[full, full, edge, edge],
        out_specs=full,
        compiler_params=pltpu.CompilerParams(vmem_limit_bytes=58 * 2**20),
        name="add_up",
    )(own, received, straight, crossed)


def local(
    visibility,
    plane_index,
    beam_index,
    strip_index,
    cell_row,
    cell_column,
    phase_index,
    kernel_table,
):
    blocks = visibility.shape[0]
    strips = lax.axis_size("tile")
    planes_band, beam_count, phase_local, row_width = kernel_table.shape
    phases = phase_local * strips
    band_index = lax.axis_index("wband")
    strip_capacity = 2 * blocks // strips
    phase_capacity = 2 * blocks // phases * phase_local
    both = phase_capacity + strip_capacity

    band = band_index.reshape(1).astype(jnp.int32)
    sizes = (strips, planes_band, beam_count, phase_local, phase_capacity, strip_capacity)
    notes, source, slot_real, slot_imag = addresses(
        sizes, band, plane_index, beam_index, strip_index, cell_row, cell_column, phase_index,
        visibility[:, 0], visibility[:, 1],
    )
    got, patches = trade(
        source, notes, kernel_table.reshape(-1, row_width), slot_real, slot_imag,
        strips, phase_capacity, strip_capacity,
    )
    cells = got.reshape(strips, both)[:, phase_capacity:].reshape(-1)
    patches = patches.reshape(-1, row_width)

    own, own_edge, other, other_edge = paint(cells, band, patches)
    received, straight, crossed = exchange_edges(strips, other, own_edge, other_edge)
    return add_up(own, received, straight, crossed)


def solution(mesh):
    placed = (
        P(("groups", "wband", "tile"), None),
        P(("groups", "wband", "tile")),
        P(("groups", "wband", "tile")),
        P(("groups", "wband", "tile")),
        P(("groups", "wband", "tile")),
        P(("groups", "wband", "tile")),
        P(("groups", "wband", "tile")),
        P("wband", None, "tile", None),
    )
    return jax.shard_map(
        local,
        mesh=mesh,
        in_specs=placed,
        out_specs=P(None, ("groups", "tile"), "wband"),
        check_vma=False,
    )
```

```python
import functools
import math

import jax
import jax.numpy as jnp
from jax import lax
from jax.experimental import pallas as pl
from jax.experimental.pallas import tpu as pltpu
from jax.sharding import PartitionSpec as P

SUP = 8
NV = 8192
ROWS = 64
LANES = 128
HALF = LANES // 2
SHIFT = 5
STRIDE = 1 << SHIFT
HEIGHT = ROWS + SUP
TILES = NV // STRIDE + 1
CHAINS = 2
MESH = pl.DeviceIdType.MESH


def rank_in_bucket(target, buckets):
    rows = target.shape[0]
    bucket = lax.broadcasted_iota(jnp.int32, (buckets, rows, LANES), 0)
    member = jnp.where(target[None] == bucket, 1.0, 0.0).reshape(buckets * rows, LANES)
    member = member.astype(jnp.bfloat16)
    up = lax.broadcasted_iota(jnp.int32, (LANES, LANES), 0)
    down = lax.broadcasted_iota(jnp.int32, (LANES, LANES), 1)
    within = jnp.dot(
        member, jnp.where(up < down, 1.0, 0.0).astype(jnp.bfloat16), preferred_element_type=jnp.float32
    )
    totals = jnp.dot(
        member, jnp.ones((LANES, LANES), jnp.bfloat16), preferred_element_type=jnp.float32
    )
    count = buckets * rows
    left = lax.broadcasted_iota(jnp.int32, (count, count), 0)
    right = lax.broadcasted_iota(jnp.int32, (count, count), 1)
    earlier = jnp.where((right < left) & (right // rows == left // rows), 1.0, 0.0)
    above = jnp.dot(
        earlier.astype(jnp.bfloat16), totals.astype(jnp.bfloat16), preferred_element_type=jnp.float32
    )
    ranks = member.astype(jnp.float32) * (within + above)
    return jnp.sum(ranks.reshape(buckets, rows, LANES), axis=0).astype(jnp.int32)


def spread_to_slots(position, total, *pieces):
    high_count = total // LANES
    high, low = position // LANES, position % LANES
    high_slot = lax.broadcasted_iota(jnp.int32, (high_count, LANES), 0)
    low_slot = lax.broadcasted_iota(jnp.int32, (LANES, LANES), 0)
    sums = jnp.zeros((len(pieces) * high_count, LANES), jnp.float32)
    for a in range(position.shape[0]):
        at_high = high[a : a + 1] == high_slot
        values = [jnp.where(at_high, piece[a : a + 1], 0.0) for piece in pieces]
        left = jnp.concatenate(values, axis=0).astype(jnp.bfloat16)
        right = jnp.where(low[a : a + 1] == low_slot, 1.0, 0.0).astype(jnp.bfloat16)
        sums = sums + lax.dot_general(
            left, right, (((1,), (1,)), ((), ())), preferred_element_type=jnp.float32
        )
    return [sums[i * high_count : (i + 1) * high_count] for i in range(len(pieces))]


def bytes_of(values):
    return [((values >> shift) & 255).astype(jnp.float32) for shift in (16, 8, 0)]


def from_bytes(top, middle, bottom):
    return (top * 65536.0 + middle * 256.0 + bottom).astype(jnp.int32)


def thirds_of(values):
    top = values.astype(jnp.bfloat16).astype(jnp.float32)
    rest = values - top
    middle = rest.astype(jnp.bfloat16).astype(jnp.float32)
    return [top, middle, rest - middle]


def address_kernel(
    sizes, band_ref, plane_ref, beam_ref, strip_ref, row_ref, column_ref, phase_ref, real_ref, imag_ref,
    notes_ref, source_ref, slot_real_ref, slot_imag_ref,
):
    strips, planes_band, beam_count, phase_local, phase_capacity, strip_capacity = sizes
    both = phase_capacity + strip_capacity
    phase, strip, column = phase_ref[...], strip_ref[...], column_ref[...]
    owner = phase // phase_local
    key = ((plane_ref[...] - band_ref[0] * planes_band) * beam_count + beam_ref[...]) * phase_local
    key = key + (phase - owner * phase_local)
    tile_row = ((column >> SHIFT) + 1) * HEIGHT + row_ref[...]
    cell = tile_row * STRIDE + (column & (STRIDE - 1))
    owner_rank = rank_in_bucket(owner, strips)
    strip_rank = rank_in_bucket(strip, strips)
    total = strips * both
    keys = spread_to_slots(owner * both + owner_rank, total, *bytes_of(key))
    cells = spread_to_slots(strip * both + phase_capacity + strip_rank, total, *bytes_of(cell))
    notes_ref[...] = from_bytes(*(k + c for k, c in zip(keys, cells)))
    slots = spread_to_slots(
        strip * strip_capacity + strip_rank,
        strips * strip_capacity,
        *bytes_of(owner * phase_capacity + owner_rank),
        *thirds_of(real_ref[...]),
        *thirds_of(imag_ref[...]),
    )
    source_ref[...] = from_bytes(*slots[:3])
    slot_real_ref[...] = slots[3] + slots[4] + slots[5]
    slot_imag_ref[...] = slots[6] + slots[7] + slots[8]


def addresses(sizes, band, *columns):
    strips, _, _, _, phase_capacity, strip_capacity = sizes
    blocks = columns[0].shape[0]
    slots = strips * strip_capacity
    vmem = pl.BlockSpec(memory_space=pltpu.VMEM)

    def shape(count, kind):
        return jax.ShapeDtypeStruct((count // LANES, LANES), kind)

    return pl.pallas_call(
        functools.partial(address_kernel, sizes),
        out_shape=(
            shape(strips * phase_capacity + slots, jnp.int32),
            shape(slots, jnp.int32),
            shape(slots, jnp.float32),
            shape(slots, jnp.float32),
        ),
        in_specs=[pl.BlockSpec(memory_space=pltpu.SMEM)] + [vmem] * len(columns),
        out_specs=(vmem,) * 4,
        compiler_params=pltpu.CompilerParams(vmem_limit_bytes=58 * 2**20),
        name="addresses",
    )(band, *(column.reshape(blocks // LANES, LANES) for column in columns))


def peer(me, step, count):
    return lax.rem(me + step + count, count)


def greet(devices):
    barrier = pltpu.get_barrier_semaphore()
    for device in devices:
        pl.semaphore_signal(barrier, inc=1, device_id=device, device_id_type=MESH)
    return barrier


def greet_tiles(me, tiles):
    barrier = pltpu.get_barrier_semaphore()

    def body(step, carry):
        pl.semaphore_signal(
            barrier, inc=1, device_id={"tile": peer(me, step, tiles)}, device_id_type=MESH
        )
        return carry

    lax.fori_loop(1, tiles, body, 0)
    return barrier


def far_first(k, tiles):
    up, down = tiles // 2 + k // 2, tiles // 2 - (k + 1) // 2
    return jnp.where(k % 2 == 0, up, down)


def trade_kernel(
    tiles, phase_capacity, strip_capacity, unroll,
    source_ref, notes_ref, table_ref, real_ref, imag_ref, got_ref, patches_ref,
    table, wide, picked, outgoing, incoming, straight, real_scale, imag_scale, chosen, leaving, listed,
    note_send, note_recv, row_send, row_recv, patch_send, patch_recv, table_sem, own_sem,
):
    me = lax.axis_index("tile")
    barrier = greet_tiles(me, tiles)
    fetch_table = pltpu.make_async_copy(table_ref, table, table_sem)
    fetch_table.start()
    pl.semaphore_wait(barrier, tiles - 1)

    def copier(source, target_ref, sends, recvs):
        def copy(step, sender):
            target = peer(me, step, tiles)
            return pltpu.make_async_remote_copy(
                src_ref=source.at[target],
                dst_ref=target_ref.at[sender],
                send_sem=sends.at[step],
                recv_sem=recvs.at[step],
                device_id={"tile": target},
                device_id_type=MESH,
            )

        return copy

    note_copy = copier(notes_ref, got_ref, note_send, note_recv)
    row_copy = copier(outgoing, incoming, row_send, row_recv)
    patch_copy = copier(leaving, patches_ref, patch_send, patch_recv)

    def start_notes(step, carry):
        note_copy(step, me).start()
        return carry

    def wait_notes(step, carry):
        note_copy(step, peer(me, -step, tiles)).wait_recv()
        return carry

    lax.fori_loop(1, tiles, start_notes, 0)
    got_ref[me] = notes_ref[me]
    fetch_table.wait()
    wide[...] = table[...].astype(jnp.float32)
    lax.fori_loop(1, tiles, wait_notes, 0)
    listing = pltpu.make_async_copy(got_ref, listed, own_sem)
    listing.start()
    listing.wait()
    groups = LANES // unroll
    group_shift = groups.bit_length() - 1

    def look_up(target):
        def body(i, carry):
            line, lane = i >> group_shift, (i & (groups - 1)) * unroll
            for u in range(unroll):
                key = listed[target, line, lane + u]
                picked[pl.ds(i * unroll + u, 1), :] = wide[pl.ds(key, 1), :]
            return carry

        lax.fori_loop(0, phase_capacity // unroll, body, 0)
        return picked[...]

    def send_rows(k, carry):
        step = far_first(k, tiles)
        target = peer(me, step, tiles)
        outgoing[target] = look_up(target).astype(jnp.bfloat16)
        row_copy(step, me).start()
        return carry

    lax.fori_loop(0, tiles - 1, send_rows, 0)

    def rows_of(tile):
        return pl.ds(pl.multiple_of(tile * phase_capacity, phase_capacity), phase_capacity)

    straight[rows_of(me), :] = look_up(me)

    def scale(g, carry):
        at = pl.ds(pl.multiple_of(g * LANES, LANES), LANES)
        for values, scales in ((real_ref, real_scale), (imag_ref, imag_scale)):
            scales[at, :] = jnp.broadcast_to(values[pl.ds(g, 1), :], (LANES, LANES)).T
        return carry

    lax.fori_loop(0, real_ref.shape[0], scale, 0)

    def take_rows(k, carry):
        step = tiles - 1 - k
        sender = peer(me, -step, tiles)
        row_copy(step, sender).wait_recv()
        straight[rows_of(sender), :] = incoming[sender].astype(jnp.float32)
        return carry

    lax.fori_loop(0, tiles - 1, take_rows, 0)
    lane_of = lax.broadcasted_iota(jnp.int32, chosen.shape, 1)

    def make(target):
        def body(i, carry):
            for u in range(unroll):
                j = i * unroll + u
                row = source_ref[target * strip_capacity + j]
                chosen[pl.ds(j, 1), :] = straight[pl.ds(row, 1), :]
            return carry

        lax.fori_loop(0, strip_capacity // unroll, body, 0)
        at = pl.ds(pl.multiple_of(target * strip_capacity, strip_capacity), strip_capacity)
        kernel = chosen[...]
        swapped = pltpu.roll(kernel, HALF, 1)
        turned = jnp.where(lane_of < HALF, -swapped, swapped)
        made = real_scale[at, :] * kernel + imag_scale[at, :] * turned
        leaving[target] = made.astype(jnp.bfloat16)

    def send_patches(k, carry):
        step = far_first(k, tiles)
        make(peer(me, step, tiles))
        patch_copy(step, me).start()
        return carry

    lax.fori_loop(0, tiles - 1, send_patches, 0)
    make(me)
    keep = pltpu.make_async_copy(leaving.at[me], patches_ref.at[me], own_sem)
    keep.start()

    def finish(step, carry):
        sender = peer(me, -step, tiles)
        note_copy(step, sender).wait_send()
        row_copy(step, sender).wait_send()
        patch_copy(step, sender).wait()
        return carry

    lax.fori_loop(1, tiles, finish, 0)
    keep.wait()


def trade(source, notes, table, real, imag, tiles, phase_capacity, strip_capacity):
    width = table.shape[1]
    notes = notes.reshape(tiles, -1, LANES)
    vmem = pl.BlockSpec(memory_space=pltpu.VMEM)
    hbm = pl.BlockSpec(memory_space=pl.ANY)
    scales = pltpu.VMEM((tiles * strip_capacity, width), jnp.float32)
    rows = pltpu.VMEM((tiles, phase_capacity, width), jnp.bfloat16)
    each = pltpu.SemaphoreType.DMA((tiles,))
    return pl.pallas_call(
        functools.partial(trade_kernel, tiles, phase_capacity, strip_capacity, 16),
        out_shape=(
            jax.ShapeDtypeStruct(notes.shape, jnp.int32),
            jax.ShapeDtypeStruct((tiles, strip_capacity, width), jnp.bfloat16),
        ),
        in_specs=[pl.BlockSpec(memory_space=pltpu.SMEM), vmem, hbm, vmem, vmem],
        out_specs=(vmem, hbm),
        scratch_shapes=[
            pltpu.VMEM(table.shape, jnp.bfloat16),
            pltpu.VMEM(table.shape, jnp.float32),
            pltpu.VMEM((phase_capacity, width), jnp.float32),
            rows,
            rows,
            pltpu.VMEM((tiles * phase_capacity, width), jnp.float32),
            scales,
            scales,
            pltpu.VMEM((strip_capacity, width), jnp.float32),
            pltpu.VMEM((tiles, strip_capacity, width), jnp.bfloat16),
            pltpu.SMEM(notes.shape, jnp.int32),
            each, each, each, each, each, each,
            pltpu.SemaphoreType.DMA,
            pltpu.SemaphoreType.DMA,
        ],
        compiler_params=pltpu.CompilerParams(
            collective_id=0, has_side_effects=True, vmem_limit_bytes=58 * 2**20
        ),
        name="trade",
    )(source.reshape(-1), notes, table, real, imag)


def edges_kernel(
    tiles, pieces, other_ref, own_edge_ref, other_edge_ref, got_ref, straight_ref, crossed_ref, sends, recvs
):
    me, band = lax.axis_index("tile"), lax.axis_index("wband")
    after, before = peer(me, 1, tiles), peer(me, -1, tiles)
    partner = {"wband": 1 - band}
    barrier = greet(
        [partner]
        + [{"wband": side, "tile": tile} for side in (band, 1 - band) for tile in (after, before)]
    )
    pl.semaphore_wait(barrier, 5)
    routes = [(own_edge_ref, straight_ref, {"tile": after})]
    routes.append((other_edge_ref, crossed_ref, {"wband": 1 - band, "tile": after}))
    rows = ROWS // pieces
    for component in range(2):
        for piece in range(pieces):
            part = (component, pl.ds(piece * rows, rows))
            routes.append((other_ref.at[part], got_ref.at[part], partner))
    copies = [
        pltpu.make_async_remote_copy(
            src_ref=source,
            dst_ref=target,
            send_sem=sends.at[n],
            recv_sem=recvs.at[n],
            device_id=device,
            device_id_type=MESH,
        )
        for n, (source, target, device) in enumerate(routes)
    ]
    for copy in copies:
        copy.start()
    for copy in copies:
        copy.wait()


def exchange_edges(tiles, other, own_edge, other_edge):
    hbm = pl.BlockSpec(memory_space=pl.ANY)
    pieces = 2
    count = 2 + 2 * pieces
    return pl.pallas_call(
        functools.partial(edges_kernel, tiles, pieces),
        out_shape=tuple(
            jax.ShapeDtypeStruct(x.shape, x.dtype) for x in (other, own_edge, other_edge)
        ),
        in_specs=[hbm] * 3,
        out_specs=(hbm,) * 3,
        scratch_shapes=[pltpu.SemaphoreType.DMA((count,)), pltpu.SemaphoreType.DMA((count,))],
        compiler_params=pltpu.CompilerParams(
            collective_id=1, has_side_effects=True, vmem_limit_bytes=58 * 2**20
        ),
        name="exchange_edges",
    )(other, own_edge, other_edge)


def paint_kernel(
    unroll, cells_ref, band_ref, patches_ref, own_ref, own_edge_ref, other_ref, other_edge_ref, wide, *canvases
):
    source = lax.broadcasted_iota(jnp.int32, (LANES, LANES), 0)
    target = lax.broadcasted_iota(jnp.int32, (LANES, LANES), 1)
    picks = [
        ((source == target + s * SUP) & (target % HALF < SUP)).astype(jnp.bfloat16) for s in range(SUP)
    ]

    chunk = math.gcd(patches_ref.shape[0], 1024)

    def open_out(i, carry):
        first = pl.multiple_of(i * chunk, chunk)
        part = patches_ref[pl.ds(first, chunk), :]
        for s in range(SUP):
            wide[pl.ds(first * SUP + s, chunk, stride=SUP), :] = jnp.dot(
                part, picks[s], preferred_element_type=jnp.float32
            )
        return carry

    lax.fori_loop(0, patches_ref.shape[0] // chunk, open_out, 0)

    def clear(i, carry):
        start = pl.multiple_of(i * HEIGHT, SUP)
        for canvas in canvases:
            canvas[pl.ds(start, HEIGHT), :] = jnp.zeros((HEIGHT, LANES), jnp.float32)
        return carry

    lax.fori_loop(0, TILES, clear, 0)

    lane = lax.broadcasted_iota(jnp.int32, (SUP, LANES), 1)

    def moved_group(i):
        spread = []
        for u in range(unroll):
            n = i * unroll + u
            patch = wide[pl.ds(pl.multiple_of(n * SUP, SUP), SUP), :]
            spread.append(pltpu.roll(patch, cells_ref[n] & (STRIDE - 1), 1))
        return tuple(spread)

    def add_group(i, spread):
        for u, moved in enumerate(spread):
            start = cells_ref[i * unroll + u] >> SHIFT
            canvas = canvases[u % len(canvases)]
            canvas[pl.ds(start, SUP), :] = canvas[pl.ds(start, SUP), :] + moved

    def body(i, spread):
        following = moved_group(i + 1)
        add_group(i, spread)
        return following

    groups = patches_ref.shape[0] // unroll
    last = lax.fori_loop(0, groups - 1, body, moved_group(0))
    add_group(groups - 1, last)

    per_block = LANES // STRIDE
    blocks = NV // LANES // 2
    lower = lane < HALF
    quarter = (lane % HALF) < STRIDE
    middle = (lane >= STRIDE) & (lane < LANES - STRIDE)

    def merge(start_block, main_ref, edge_ref):
        def column(b, carry):
            first = (start_block + b) * per_block
            at = pl.ds(pl.multiple_of(b * LANES, LANES), LANES)
            merged = []
            for p in range(HEIGHT // SUP):
                tiles = []
                for t in range(per_block + 1):
                    where = pl.ds(pl.multiple_of((first + t) * HEIGHT + p * SUP, SUP), SUP)
                    tile = canvases[0][where, :]
                    for canvas in canvases[1:]:
                        tile = tile + canvas[where, :]
                    tiles.append(tile)
                before, t0, t1, t2, t3 = tiles
                edges = jnp.where(quarter, t3, before)
                real = jnp.where(lower, t0, pltpu.roll(t2, HALF, 1)) + jnp.where(
                    middle, pltpu.roll(t1, STRIDE, 1), pltpu.roll(edges, LANES - STRIDE, 1)
                )
                imag = jnp.where(lower, pltpu.roll(t0, HALF, 1), t2) + jnp.where(
                    middle, pltpu.roll(t1, LANES - STRIDE, 1), pltpu.roll(edges, STRIDE, 1)
                )
                merged.append((real, imag))
            for p in range(0, ROWS // SUP, 2):
                rows = slice(p * SUP, (p + 2) * SUP)
                for k in range(2):
                    pair = jnp.concatenate([merged[p][k], merged[p + 1][k]], axis=0)
                    main_ref[k, rows, at] = pair.astype(main_ref.dtype)
            edge_ref[:, at] = jnp.concatenate(merged[-1], axis=0).astype(edge_ref.dtype)
            return carry

        lax.fori_loop(0, blocks, column, 0, unroll=4)

    band = band_ref[0]
    merge(band * blocks, own_ref, own_edge_ref)
    merge((1 - band) * blocks, other_ref, other_edge_ref)


def paint(cells, band, patches):
    main = jax.ShapeDtypeStruct((2, ROWS, NV // 2), jnp.float32)
    other = jax.ShapeDtypeStruct(main.shape, jnp.bfloat16)
    edge = jax.ShapeDtypeStruct((2 * SUP, NV // 2), jnp.bfloat16)
    smem = pl.BlockSpec(memory_space=pltpu.SMEM)
    vmem = pl.BlockSpec(memory_space=pltpu.VMEM)
    return pl.pallas_call(
        functools.partial(paint_kernel, 128),
        out_shape=(main, edge, other, edge),
        in_specs=[smem, smem, vmem],
        out_specs=(vmem, vmem, vmem, vmem),
        scratch_shapes=[pltpu.VMEM((patches.shape[0] * SUP, LANES), jnp.float32)]
        + [pltpu.VMEM((TILES * HEIGHT, LANES), jnp.float32)] * CHAINS,
        compiler_params=pltpu.CompilerParams(vmem_limit_bytes=56 * 2**20),
        name="paint",
    )(cells, band, patches)


def add_up_kernel(own_ref, received_ref, straight_ref, crossed_ref, out_ref):
    out_ref[...] = own_ref[...] + received_ref[...].astype(jnp.float32)
    lower_edge = (pl.program_id(1) == 0) & (lax.axis_index("tile") > 0)

    @pl.when(lower_edge)
    def _():
        edge = straight_ref[...].astype(jnp.float32) + crossed_ref[...].astype(jnp.float32)
        edge = jnp.where(pl.program_id(0) == 0, edge[:SUP], edge[SUP:])
        out_ref[0, :SUP, :] = out_ref[0, :SUP, :] + edge


def add_up(own, received, straight, crossed):
    rows, columns = ROWS // 2, own.shape[2]
    part = pl.BlockSpec((1, rows, columns), lambda k, r: (k, r, 0))
    edge = pl.BlockSpec((2 * SUP, columns), lambda k, r: (0, 0))
    return pl.pallas_call(
        add_up_kernel,
        out_shape=jax.ShapeDtypeStruct(own.shape, own.dtype),
        grid=(2, ROWS // rows),
        in_specs=[part, part, edge, edge],
        out_specs=part,
        compiler_params=pltpu.CompilerParams(vmem_limit_bytes=58 * 2**20),
        name="add_up",
    )(own, received, straight, crossed)


def local(
    visibility,
    plane_index,
    beam_index,
    strip_index,
    cell_row,
    cell_column,
    phase_index,
    kernel_table,
):
    blocks = visibility.shape[0]
    strips = lax.axis_size("tile")
    planes_band, beam_count, phase_local, row_width = kernel_table.shape
    phases = phase_local * strips
    band_index = lax.axis_index("wband")
    strip_capacity = 2 * blocks // strips
    phase_capacity = 2 * blocks // phases * phase_local
    both = phase_capacity + strip_capacity

    band = band_index.reshape(1).astype(jnp.int32)
    sizes = (strips, planes_band, beam_count, phase_local, phase_capacity, strip_capacity)
    notes, source, slot_real, slot_imag = addresses(
        sizes, band, plane_index, beam_index, strip_index, cell_row, cell_column, phase_index,
        visibility[:, 0], visibility[:, 1],
    )
    got, patches = trade(
        source, notes, kernel_table.reshape(-1, row_width), slot_real, slot_imag,
        strips, phase_capacity, strip_capacity,
    )
    cells = got.reshape(strips, both)[:, phase_capacity:].reshape(-1)
    patches = patches.reshape(-1, row_width)

    own, own_edge, other, other_edge = paint(cells, band, patches)
    received, straight, crossed = exchange_edges(strips, other, own_edge, other_edge)
    return add_up(own, received, straight, crossed)


def solution(mesh):
    placed = (
        P(("groups", "wband", "tile"), None),
        P(("groups", "wband", "tile")),
        P(("groups", "wband", "tile")),
        P(("groups", "wband", "tile")),
        P(("groups", "wband", "tile")),
        P(("groups", "wband", "tile")),
        P(("groups", "wband", "tile")),
        P("wband", None, "tile", None),
    )
    return jax.shard_map(
        local,
        mesh=mesh,
        in_specs=placed,
        out_specs=P(None, ("groups", "tile"), "wband"),
        check_vma=False,
    )
```
